512 devices in a mesh: dp: 8 (over y), row: 8 (over z_lo, core), col: 8 (over z_hi, x).
Axes of the slice: x: 4, y: 8, z: 8 (z_hi: 2, z_lo: 4; z = z_hi * 4 + z_lo), core: 2. Of those that a mesh axis runs over, the one named last changes fastest.
Arguments:
- block_input: bfloat16 [8, 128, 256, 192], P('dp', 'row', 'col'), may hold values from -6 to 6
- grad_out: bfloat16 [8, 128, 256, 192], P('dp', 'row', 'col'), may hold values from -6 to 6
- region_ids: int32 [128, 256], P('row', 'col'), may hold values from 0 to 9, as said below
- layernorm_scale: float32 [192], replicated, may hold values from 0.25 to 1.75
- layernorm_bias: float32 [192], replicated, may hold values from -3 to 3
- qkv_weight: bfloat16 [192, 576], replicated, may hold values from -0.4375 to 0.4375
- qkv_bias: float32 [576], replicated, may hold values from -3 to 3
- proj_weight: bfloat16 [192, 192], replicated, may hold values from -0.4375 to 0.4375
- bias_table: float32 [225, 6], replicated, may hold values from -4 to 4
- position_index: int32 [64, 64], replicated, may hold values from 0 to 224, as said below
Outputs:
- grad_x: bfloat16 [8, 128, 256, 192], P('dp', 'row', 'col')
- grad_qkv_weight: float32 [192, 576], replicated
- grad_qkv_bias: float32 [576], replicated
- grad_proj_weight: float32 [192, 192], replicated
- grad_proj_bias: float32 [192], replicated
- gradient_norm_scale: float32 [192], replicated
- grad_norm_bias: float32 [192], replicated
- grad_table: float32 [225, 6], replicated
The draws below stay inside these ranges and needn't reach their ends.
Inputs may be any that keep to these rules, and one draw needn't show every extreme that they name: `region_ids`: each id marks one region of the shifted image. The regions are the three row bands split at 120 and 124, crossed with the three column bands split at 248 and 252, plus one region of padded pixels. The padded pixels are 1 to 3 rows just before row 124 and 1 to 3 columns just before column 252. Every window outside the last window row and column of the image holds a single id. `position_index`: pixel pairs of a window with the same row offset and the same column offset share an entry; distinct offset pairs have distinct entries.
All inputs are finite; a program needn't handle non-finite values.
Results may differ from the reference program's by a relative error of at most 0.011.
Values may be sent and summed in bfloat16 or wider, within the bound.
No kernel may reach another device: no remote copies, remote signals or barrier semaphores. Data moves between devices by JAX's collectives and lax.ppermute only.
A program may use at most 64 MiB of HBM per device.

```python
import jax
import jax.numpy as jnp
from jax import lax

C = 192
HEADS = 6
WIN = 8
SHIFT = 4
TOKENS_WIN = 64
TABLE = 225
FRAMES = 8
HEIGHT = 128
WIDTH = 256


def band_of(places, length):
    return jnp.where(places < length - WIN, 0, jnp.where(places < length - SHIFT, 1, 2)).astype(jnp.int32)


def draw_region_ids(key, part):
    key = jax.random.fold_in(key, 11)
    key_rows, key_cols, key_labels = jax.random.split(key, 3)
    pad_rows = jax.random.randint(key_rows, (), 1, SHIFT, dtype=jnp.int32)
    pad_cols = jax.random.randint(key_cols, (), 1, SHIFT, dtype=jnp.int32)
    rows = jnp.arange(HEIGHT, dtype=jnp.int32)
    cols = jnp.arange(WIDTH, dtype=jnp.int32)
    regions = 3 * band_of(rows, HEIGHT)[:, None] + band_of(cols, WIDTH)[None, :]
    row_pad = (rows >= HEIGHT - SHIFT - pad_rows) & (rows < HEIGHT - SHIFT)
    col_pad = (cols >= WIDTH - SHIFT - pad_cols) & (cols < WIDTH - SHIFT)
    padded = row_pad[:, None] | col_pad[None, :]
    regions = jnp.where(padded, 9, regions).astype(jnp.int32)
    labels = jax.random.permutation(key_labels, 10).astype(jnp.int32)
    return labels[regions].astype(jnp.int32)


def draw_position_index(key, part):
    key = jax.random.fold_in(key, 12)
    order = jax.random.permutation(key, TABLE).astype(jnp.int32)
    places = jnp.arange(TOKENS_WIN, dtype=jnp.int32)
    row_in = places // WIN
    col_in = places % WIN
    relative = (row_in[:, None] - row_in[None, :] + WIN - 1) * (2 * WIN - 1) + (col_in[:, None] - col_in[None, :] + WIN - 1)
    return order[relative].astype(jnp.int32)


def level_of(rng, shape, shards, least, top_value):
    loudness, own = 1.0, jax.random.fold_in(rng, 6)
    for axis_at, parts in shards:
        heights = jnp.exp(jax.random.uniform(jax.random.fold_in(own, axis_at), (parts,), jnp.float32, least / len(shards), top_value / len(shards)))
        loudness = loudness * jnp.repeat(heights, shape[axis_at] // parts).reshape([-1 if axis == axis_at else 1 for axis in range(len(shape))])
    return loudness


def gaussian(own_key, shape, deviation, bound, pieces=(), kind=jnp.bfloat16):
    array = deviation * jax.random.normal(own_key, shape, jnp.float32)
    if pieces:
        array = array * level_of(own_key, shape, pieces, -0.22, 0.18)
    return jnp.clip(array, -bound, bound).astype(kind)


def setup_inputs(seed: int = 0) -> dict:
    arg_keys = jax.random.split(jax.random.key(seed), 11)
    block_input = gaussian(arg_keys[0], (FRAMES, HEIGHT, WIDTH, C), 1.0, 6.0, ((0, 8), (1, 8), (2, 8)))
    grad_out = gaussian(arg_keys[1], (FRAMES, HEIGHT, WIDTH, C), 1.0, 6.0, ((0, 8), (1, 8), (2, 8)))
    region_ids = draw_region_ids(jax.random.fold_in(arg_keys[10], 71), 0)
    layernorm_scale = jnp.clip(1.0 + 0.15 * jax.random.normal(arg_keys[3], (C,), jnp.float32), 0.25, 1.75)
    layernorm_bias = gaussian(arg_keys[4], (C,), 0.5, 3.0, (), jnp.float32)
    qkv_weight = gaussian(arg_keys[5], (C, 3 * C), C ** -0.5, 0.4375)
    qkv_bias = gaussian(arg_keys[6], (3 * C,), 0.5, 3.0, (), jnp.float32)
    proj_weight = gaussian(arg_keys[7], (C, C), C ** -0.5, 0.4375)
    bias_table = gaussian(arg_keys[8], (TABLE, HEADS), 1.0, 4.0, (), jnp.float32)
    position_index = draw_position_index(jax.random.fold_in(arg_keys[10], 71), 0)
    return dict(block_input=block_input, grad_out=grad_out, region_ids=region_ids, layernorm_scale=layernorm_scale, layernorm_bias=layernorm_bias, qkv_weight=qkv_weight, qkv_bias=qkv_bias, proj_weight=proj_weight, bias_table=bias_table, position_index=position_index)


def windows(a):
    frames, height, width, chan = a.shape
    a = a.reshape(frames, height // WIN, WIN, width // WIN, WIN, chan)
    return a.transpose(0, 1, 3, 2, 4, 5).reshape(-1, WIN * WIN, chan)

def unwindows(a, frames, height, width):
    chan = a.shape[-1]
    a = a.reshape(frames, height // WIN, width // WIN, WIN, WIN, chan)
    return a.transpose(0, 1, 3, 2, 4, 5).reshape(frames, height, width, chan)

def local_grads(shifted_x, shifted_grad, region_ids, layernorm_scale, layernorm_bias, qkv_weight, qkv_bias, proj_weight, bias_table, position_index):
    frames, height, width, chan = shifted_x.shape
    heads = bias_table.shape[1]
    head_dim = chan // heads
    count = position_index.shape[0]
    scale = head_dim ** (-0.5)
    input_float = shifted_x.astype(jnp.float32)
    mean_x = lax.optimization_barrier(jnp.mean(input_float, -1, keepdims=True))
    centered_input = input_float - mean_x
    reciprocal_deviation = lax.rsqrt(lax.optimization_barrier(jnp.mean(centered_input * centered_input, -1, keepdims=True)) + 1e-05)
    standardized_input = centered_input * reciprocal_deviation
    normalized_rows = (standardized_input * layernorm_scale + layernorm_bias).astype(jnp.bfloat16)
    normed_rows = windows(normalized_rows).reshape(-1, chan)
    grad_rows = windows(shifted_grad).reshape(-1, chan)
    qkv = jnp.dot(normed_rows, qkv_weight, preferred_element_type=jnp.float32) + qkv_bias
    qkv = qkv.reshape(-1, count, 3, heads, head_dim)
    query = (qkv[:, :, 0] * scale).astype(jnp.bfloat16).transpose(0, 2, 1, 3)
    key = qkv[:, :, 1].astype(jnp.bfloat16).transpose(0, 2, 1, 3)
    value = qkv[:, :, 2].astype(jnp.bfloat16).transpose(0, 2, 1, 3)
    onehot = (position_index.reshape(-1)[:, None] == jnp.arange(bias_table.shape[0], dtype=jnp.int32)[None, :]).astype(jnp.float32)
    bias = jnp.dot(onehot, bias_table, precision=lax.Precision.HIGHEST).reshape(count, count, heads).transpose(2, 0, 1)
    ids = windows(jnp.broadcast_to(region_ids[None, :, :, None], (1, height, width, 1))).reshape(-1, count)
    ids = jnp.tile(ids, (frames, 1))
    mask = jnp.where(ids[:, :, None] == ids[:, None, :], 0.0, -100.0).astype(jnp.float32)
    scores = jnp.einsum('whqd,whkd->whqk', query.astype(jnp.float32), key.astype(jnp.float32))
    scores = scores + bias[None] + mask[:, None]
    probs = jax.nn.softmax(scores, axis=-1)
    probs_b = probs.astype(jnp.bfloat16)
    attn = jnp.einsum('whqk,whkd->whqd', probs_b.astype(jnp.float32), value.astype(jnp.float32)).astype(jnp.bfloat16)
    attn_rows = attn.transpose(0, 2, 1, 3).reshape(-1, chan)
    grad_proj_weight = jnp.dot(attn_rows.T, grad_rows, preferred_element_type=jnp.float32)
    grad_proj_bias = lax.optimization_barrier(jnp.sum(grad_rows.astype(jnp.float32), 0))
    d_attn = jnp.dot(grad_rows, proj_weight.T, preferred_element_type=jnp.float32).astype(jnp.bfloat16)
    d_attn = d_attn.reshape(-1, count, heads, head_dim).transpose(0, 2, 1, 3)
    d_p = jnp.einsum('whqd,whkd->whqk', d_attn.astype(jnp.float32), value.astype(jnp.float32))
    d_v = jnp.einsum('whqk,whqd->whkd', probs_b.astype(jnp.float32), d_attn.astype(jnp.float32)).astype(jnp.bfloat16)
    d_s = probs * (d_p - lax.optimization_barrier(jnp.sum(d_p * probs, -1, keepdims=True)))
    d_bias = lax.optimization_barrier(jnp.sum(d_s, 0)).transpose(1, 2, 0).reshape(count * count, heads)
    grad_table = jnp.dot(onehot.T, d_bias, precision=lax.Precision.HIGHEST)
    d_sb = d_s.astype(jnp.bfloat16)
    d_q = (jnp.einsum('whqk,whkd->whqd', d_sb.astype(jnp.float32), key.astype(jnp.float32)) * scale).astype(jnp.bfloat16)
    d_k = jnp.einsum('whqk,whqd->whkd', d_sb.astype(jnp.float32), query.astype(jnp.float32)).astype(jnp.bfloat16)
    d_qkv = jnp.stack([d_q, d_k, d_v]).transpose(1, 3, 0, 2, 4).reshape(-1, 3 * chan)
    grad_qkv_weight = jnp.dot(normed_rows.T, d_qkv, preferred_element_type=jnp.float32)
    grad_qkv_bias = lax.optimization_barrier(jnp.sum(d_qkv.astype(jnp.float32), 0))
    grad_normalized = jnp.dot(d_qkv, qkv_weight.T, preferred_element_type=jnp.float32)
    grad_normalized = unwindows(grad_normalized.reshape(-1, count, chan), frames, height, width)
    gradient_norm_scale = lax.optimization_barrier(jnp.sum(grad_normalized * standardized_input, (0, 1, 2)))
    grad_norm_bias = lax.optimization_barrier(jnp.sum(grad_normalized, (0, 1, 2)))
    grad_standardized = grad_normalized * layernorm_scale
    grad_displaced = reciprocal_deviation * (grad_standardized - lax.optimization_barrier(jnp.mean(grad_standardized, -1, keepdims=True)) - standardized_input * lax.optimization_barrier(jnp.mean(grad_standardized * standardized_input, -1, keepdims=True)))
    return (grad_displaced, (grad_qkv_weight, grad_qkv_bias, grad_proj_weight, grad_proj_bias, gradient_norm_scale, grad_norm_bias, grad_table))

def reference(block_input, grad_out, region_ids, layernorm_scale, layernorm_bias, qkv_weight, qkv_bias, proj_weight, bias_table, position_index):
    shifted_x = jnp.roll(block_input, (-SHIFT, -SHIFT), (1, 2))
    shifted_grad = jnp.roll(grad_out, (-SHIFT, -SHIFT), (1, 2))

    def one_frame(pair):
        frame_x, frame_grad = pair
        return local_grads(frame_x[None], frame_grad[None], region_ids, layernorm_scale, layernorm_bias, qkv_weight, qkv_bias, proj_weight, bias_table, position_index)
    grad_displaced, grads = lax.map(one_frame, (shifted_x, shifted_grad))
    grads = jax.tree.map(lambda grad_part: lax.optimization_barrier(jnp.sum(grad_part, 0)), grads)
    back = jnp.roll(grad_displaced[:, 0], (SHIFT, SHIFT), (1, 2))
    grad_x = (grad_out.astype(jnp.float32) + back).astype(jnp.bfloat16)
    return (grad_x, grads[0], grads[1], grads[2], grads[3], grads[4], grads[5], grads[6])
```

```python
import jax
import jax.numpy as jnp
from jax import lax
from jax.experimental import pallas as pl
from jax.experimental.pallas import tpu as pltpu
from jax.sharding import Mesh, PartitionSpec as P

WIN = 8
SHIFT = 4
TOK = 64
HEADS = 6
CHAN = 192
DIM = 32
ROWS = 16
COLS = 32
TABLE = 225
OFF = 256
CHUNKS = 32
PACK = 40
BF = jnp.bfloat16
F32 = jnp.float32
HIGH = lax.Precision.HIGHEST

FIRST = ("y", "x")
SECOND = ("zl", "c", "zh")
ROW = ("zl", "c")
COL = ("zh", "x")


def nn(a, b, precision=None):
    return lax.dot_general(a, b, (((1,), (0,)), ((), ())), precision=precision, preferred_element_type=F32)


def nt(a, b, precision=None):
    return lax.dot_general(a, b, (((1,), (1,)), ((), ())), precision=precision, preferred_element_type=F32)


def tn(a, b, precision=None):
    return lax.dot_general(a, b, (((0,), (0,)), ((), ())), precision=precision, preferred_element_type=F32)


def iota(shape, dim):
    return lax.broadcasted_iota(jnp.int32, shape, dim)


def spread_reversed():
    a, lane = iota((TOK, 128), 0), iota((TOK, 128), 1)
    return (lane == 127 - (16 * (a // WIN) + a % WIN)).astype(F32)


def squeeze_pair():
    source, lane = iota((256, 128), 0), iota((256, 128), 1)
    head, a = lane // TOK, lane % TOK
    return (source == 128 * head + 16 * (a // WIN) + a % WIN).astype(F32)


def offset_sums(spread):
    wide = jnp.concatenate([spread, jnp.zeros((TOK, 128), F32)], axis=1)
    total = jnp.zeros((WIN, OFF), F32)
    for i in range(WIN):
        total += pltpu.roll(wide[WIN * i : WIN * i + WIN], 16 * i, 1, stride=1, stride_axis=0)
    return jnp.sum(total, 0, keepdims=True)


def prepare_kernel(pos_ref, table_ref, bias_ref, perm_ref, pad_ref):
    pos = pos_ref[...].astype(F32)
    rev = spread_reversed()
    count = offset_sums(nn(jnp.ones((TOK, TOK), F32), rev))
    entry_ahead = offset_sums(nn(pos, rev, HIGH))
    entry_back = offset_sums(nn(pos.T, rev, HIGH))

    def entry(total):
        whole = jnp.floor(total / jnp.maximum(count, 1.0) + 0.5).astype(jnp.int32)
        return jnp.where(count > 0.5, whole, -1)

    t = iota((OFF, OFF), 0)
    perm_ref[...] = (t == entry(entry_back)).astype(F32)
    perm_ahead = (t == entry(entry_ahead)).astype(F32)
    pad_ref[...] = jnp.zeros_like(pad_ref)
    pad_ref[0:TABLE, 0:HEADS] = table_ref[...]
    by_offset = nn(pad_ref[...].T[0:8], perm_ahead, HIGH)
    squeeze = squeeze_pair()
    for pair in range(HEADS // 2):
        halves = []
        for h in (2 * pair, 2 * pair + 1):
            line = jnp.broadcast_to(by_offset[h : h + 1], (WIN, OFF))
            halves.append(
                jnp.concatenate(
                    [
                        pltpu.roll(line, 16 * i + 129, 1, stride=1, stride_axis=0)[:, 0:128]
                        for i in range(WIN)
                    ],
                    axis=0,
                )
            )
        bias_ref[:, 128 * pair : 128 * pair + 128] = nn(
            jnp.concatenate(halves, axis=1), squeeze, HIGH
        )


def main_kernel(
    x_ref,
    g_ref,
    row_ref,
    col_ref,
    corner_ref,
    ids_ref,
    ls_ref,
    lb_ref,
    w_ref,
    qb_ref,
    wp_ref,
    bias_ref,
    perm_ref,
    ds_ref,
    edge_ref,
    pack_ref,
    ext_ref,
    xhat_ref,
    rstd_ref,
    normed_ref,
    grad_ref,
    q_ref,
    k_ref,
    v_ref,
    da_ref,
    attn_ref,
    dq_ref,
    dk_ref,
    dv_ref,
):
    scale = DIM ** (-0.5)

    def windowed(tile_ref, which):
        ext_ref[0:ROWS, 0:COLS, :] = tile_ref[...].astype(F32)
        ext_ref[ROWS : ROWS + SHIFT, 0:COLS, :] = row_ref[which].astype(F32)
        ext_ref[0:ROWS, COLS : COLS + SHIFT, :] = col_ref[which].astype(F32)
        ext_ref[ROWS : ROWS + SHIFT, COLS : COLS + SHIFT, :] = corner_ref[which].astype(F32)
        pieces = []
        for wr in range(ROWS // WIN):
            for wc in range(COLS // WIN):
                r, c = WIN * wr + SHIFT, WIN * wc + SHIFT
                pieces.append(ext_ref[r : r + WIN, c : c + WIN, :].reshape(TOK, CHAN))
        return jnp.concatenate(pieces, axis=0)

    grad = windowed(g_ref, 1)
    grad_ref[...] = grad.astype(BF)
    grad_proj_bias = jnp.sum(grad, 0, keepdims=True)
    x = windowed(x_ref, 0)
    mean = jnp.sum(x, -1, keepdims=True) * (1.0 / CHAN)
    centered = x - mean
    rstd = lax.rsqrt(jnp.sum(centered * centered, -1, keepdims=True) * (1.0 / CHAN) + 1e-05)
    xhat = centered * rstd
    xhat_ref[...] = xhat
    rstd_ref[...] = rstd
    normed = (xhat * ls_ref[...] + lb_ref[...]).astype(BF)
    normed_ref[...] = normed
    w = w_ref[...]
    w_q, w_k, w_v = w[:, 0:CHAN], w[:, CHAN : 2 * CHAN], w[:, 2 * CHAN : 3 * CHAN]
    qb = qb_ref[...]
    q_ref[...] = ((nn(normed, w_q) + qb[:, 0:CHAN]) * scale).astype(BF)
    k_ref[...] = (nn(normed, w_k) + qb[:, CHAN : 2 * CHAN]).astype(BF)
    v_ref[...] = (nn(normed, w_v) + qb[:, 2 * CHAN : 3 * CHAN]).astype(BF)
    da_ref[...] = nt(grad_ref[...], wp_ref[...]).astype(BF)

    token, tile_row = iota((8 * TOK, ROWS), 0), iota((8 * TOK, ROWS), 1)
    window, inside = token // TOK, token % TOK
    pick_row = (tile_row == WIN * (window // 4) + inside // WIN).astype(BF)
    spread_ids = nn(pick_row, ids_ref[...].astype(F32).astype(BF))
    token, tile_col = iota((8 * TOK, COLS), 0), iota((8 * TOK, COLS), 1)
    window, inside = token // TOK, token % TOK
    pick_col = tile_col == WIN * (window % 4) + inside % WIN
    ids = jnp.sum(jnp.where(pick_col, spread_ids, 0.0), -1, keepdims=True)
    region = (ids == iota((8 * TOK, 16), 1).astype(F32)).astype(BF)

    head_of = iota((TOK, CHAN), 1) // DIM

    def by_head(a):
        zero = jnp.zeros_like(a)
        return jnp.concatenate([jnp.where(head_of == h, a, zero) for h in range(HEADS)], axis=0)

    def own_head(a):
        total = jnp.where(head_of == 0, a[0:TOK], 0.0)
        for h in range(1, HEADS):
            total = jnp.where(head_of == h, a[TOK * h : TOK * h + TOK], total)
        return total

    d_sum = jnp.zeros((TOK, HEADS * TOK), F32)
    for win in range(8):
        s = slice(TOK * win, TOK * win + TOK)
        q_heads = by_head(q_ref[s])
        key = k_ref[s]
        value = v_ref[s]
        same = nt(region[s], jnp.concatenate([region[s]] * HEADS, axis=0))
        scores = nt(key, q_heads) + bias_ref[...] + (same - 1.0) * 100.0
        top = jnp.max(scores, 0, keepdims=True)
        e = jnp.exp(scores - top)
        p = e * (1.0 / jnp.sum(e, 0, keepdims=True))
        pb = p.astype(BF)
        attn_ref[s] = own_head(tn(pb, value)).astype(BF)
        da_heads = by_head(da_ref[s])
        d_p = nt(value, da_heads)
        dv_ref[s] = nn(pb, da_heads).astype(BF)
        d_s = p * (d_p - jnp.sum(d_p * p, 0, keepdims=True))
        d_sum += d_s
        d_sb = d_s.astype(BF)
        dq_ref[s] = (own_head(tn(d_sb, key)) * scale).astype(BF)
        dk_ref[s] = nn(d_sb, q_heads).astype(BF)

    rev = spread_reversed()
    lines = [
        offset_sums(nn(d_sum[:, TOK * h : TOK * h + TOK], rev, HIGH)) for h in range(HEADS)
    ]
    lines += [jnp.zeros((1, OFF), F32)] * 2
    by_entry = nt(jnp.concatenate(lines, axis=0), perm_ref[...], HIGH)

    dq, dk, dv = dq_ref[...], dk_ref[...], dv_ref[...]
    d_normed = nt(dq, w_q) + nt(dk, w_k) + nt(dv, w_v)
    xhat = xhat_ref[...]
    norm_scale = jnp.sum(d_normed * xhat, 0, keepdims=True)
    norm_bias = jnp.sum(d_normed, 0, keepdims=True)
    d_hat = d_normed * ls_ref[...]
    mean_hat = jnp.sum(d_hat, -1, keepdims=True) * (1.0 / CHAN)
    mean_mix = jnp.sum(d_hat * xhat, -1, keepdims=True) * (1.0 / CHAN)
    d_shifted = rstd_ref[...] * (d_hat - mean_hat - xhat * mean_mix)
    for win in range(8):
        wr, wc = win // 4, win % 4
        block = d_shifted[TOK * win : TOK * win + TOK].reshape(WIN, WIN, CHAN)
        ds_ref[WIN * wr : WIN * wr + WIN, WIN * wc : WIN * wc + WIN, :] = block
    edge_ref[...] = ds_ref[ROWS - SHIFT : ROWS].astype(BF)

    normed = normed_ref[...]
    weights = jnp.concatenate(
        [tn(normed, dq), tn(normed, dk), tn(normed, dv), tn(attn_ref[...], grad_ref[...])], axis=1
    )
    sums = [jnp.sum(a.astype(F32), 0, keepdims=True) for a in (dq, dk, dv)] + [grad_proj_bias]
    small = jnp.concatenate(
        [
            jnp.concatenate(sums, axis=1),
            jnp.concatenate([norm_scale, norm_bias, jnp.zeros((1, 2 * CHAN), F32)], axis=1),
            jnp.concatenate([by_entry[0:1], by_entry[1:2], by_entry[2:3]], axis=1),
            jnp.concatenate([by_entry[3:4], by_entry[4:5], by_entry[5:6]], axis=1),
        ],
        axis=0,
    )
    high = small.astype(BF).astype(F32)
    small = jnp.concatenate([high, small - high], axis=0)
    packed = jnp.concatenate([weights, small], axis=0)
    for chunk in range(CHUNKS):
        tiles = []
        for tile in range(5 * chunk, 5 * chunk + 5):
            r, c = tile // 6, tile % 6
            if r < 25:
                tiles.append(packed[8 * r : 8 * r + 8, 128 * c : 128 * c + 128])
            else:
                tiles.append(jnp.zeros((8, 128), F32))
        pack_ref[chunk] = jnp.concatenate(tiles, axis=0).astype(BF)


def add_up(ref, count):
    total = ref[0].astype(F32)
    for i in range(1, count):
        total += ref[i].astype(F32)
    return total


def sum_kernel(got_ref, out_ref):
    total = add_up(got_ref, got_ref.shape[0]).astype(BF)
    for i in range(out_ref.shape[0]):
        out_ref[i] = total


def unpack_kernel(got_ref, w_ref, wb_ref, p_ref, pb_ref, ns_ref, nb_ref, table_ref, all_ref):
    for tile in range(150):
        r, c = tile // 6, tile % 6
        if tile % 5 == 0:
            chunk = got_ref[tile // 5].astype(F32)
        part = 8 * (tile % 5)
        all_ref[8 * r : 8 * r + 8, 128 * c : 128 * c + 128] = chunk[part : part + 8]
    w_ref[...] = all_ref[0:CHAN, 0 : 3 * CHAN]
    p_ref[...] = all_ref[0:CHAN, 3 * CHAN : 4 * CHAN]
    small = all_ref[CHAN : CHAN + 4, :] + all_ref[CHAN + 4 : CHAN + 8, :]
    wb_ref[...] = small[0:1, 0 : 3 * CHAN]
    pb_ref[...] = small[0:1, 3 * CHAN : 4 * CHAN]
    ns_ref[...] = small[1:2, 0:CHAN]
    nb_ref[...] = small[1:2, CHAN : 2 * CHAN]
    lines = [small[2 + h // 3 : 3 + h // 3, OFF * (h % 3) : OFF * (h % 3) + OFF] for h in range(HEADS)]
    lines += [jnp.zeros((1, OFF), F32)] * 2
    table = jnp.concatenate(lines, axis=0).T
    table_ref[...] = table[0:TABLE, 0:HEADS]


def kernel_call(kernel, out_shape, scratch=(), flops=10**7):
    return pl.pallas_call(
        kernel,
        out_shape=out_shape,
        scratch_shapes=scratch,
        cost_estimate=pl.CostEstimate(flops=flops, bytes_accessed=10**6, transcendentals=0),
        compiler_params=pltpu.CompilerParams(vmem_limit_bytes=40 * 2**20),
    )


def shape(dims, kind=F32):
    return jax.ShapeDtypeStruct(dims, kind)


def moved(block, axes, distance):
    sizes = [lax.axis_size(a) for a in axes]
    count = sizes[0] * sizes[1]
    return lax.ppermute(block, axes, [((i - distance) % count, i) for i in range(count)])


def moved_corner(block):
    pairs = [
        (8 * ((r + 1) % 8) + (c + 1) % 8, 8 * r + c) for r in range(8) for c in range(8)
    ]
    return lax.ppermute(block, ROW + COL, pairs)


def prepare(position_index, bias_table):
    return kernel_call(
        prepare_kernel,
        (shape((TOK, HEADS * TOK)), shape((OFF, OFF))),
        [pltpu.VMEM((OFF, 128), F32)],
    )(position_index, bias_table)


def main(*args):
    tokens = 8 * TOK
    return kernel_call(
        main_kernel,
        (
            shape((ROWS, COLS, CHAN)),
            shape((SHIFT, COLS, CHAN), BF),
            shape((CHUNKS, PACK, 128), BF),
        ),
        [
            pltpu.VMEM((ROWS + 8, COLS + 8, CHAN), F32),
            pltpu.VMEM((tokens, CHAN), F32),
            pltpu.VMEM((tokens, 1), F32),
        ]
        + [pltpu.VMEM((tokens, CHAN), BF)] * 10,
        flops=10**9,
    )(*args)


def unpack(gathered):
    return kernel_call(
        unpack_kernel,
        (
            shape((CHAN, 3 * CHAN)),
            shape((1, 3 * CHAN)),
            shape((CHAN, CHAN)),
            shape((1, CHAN)),
            shape((1, CHAN)),
            shape((1, CHAN)),
            shape((TABLE, HEADS)),
        ),
        [pltpu.VMEM((CHAN + 8, 4 * CHAN), F32)],
    )(gathered)


def on_device(
    block_input,
    grad_out,
    region_ids,
    layernorm_scale,
    layernorm_bias,
    qkv_weight,
    qkv_bias,
    proj_weight,
    bias_table,
    position_index,
):
    x, g = block_input[0], grad_out[0]
    row = moved(jnp.stack([x[:SHIFT], g[:SHIFT]]), ROW, -1)
    col = moved(jnp.stack([x[:, :SHIFT], g[:, :SHIFT]]), COL, -1)
    corner = moved_corner(jnp.stack([x[:SHIFT, :SHIFT], g[:SHIFT, :SHIFT]]))
    bias, perm = prepare(position_index, bias_table)
    d_shifted, edge, packed = main(
        x,
        g,
        row,
        col,
        corner,
        region_ids,
        layernorm_scale[None],
        layernorm_bias[None],
        qkv_weight,
        qkv_bias[None],
        proj_weight,
        bias,
        perm,
    )
    above = moved(edge, ROW, 1)
    got = lax.all_to_all(packed, FIRST, 0, 0, tiled=True)
    part = kernel_call(sum_kernel, shape((16, PACK, 128), BF))(got)
    back = jnp.concatenate([above.astype(F32), d_shifted[: ROWS - SHIFT]], axis=0)
    left = moved(back[:, COLS - SHIFT :].astype(BF), COL, 1)
    got = lax.all_to_all(part, SECOND, 0, 0, tiled=True)
    whole = kernel_call(sum_kernel, shape((CHUNKS, PACK, 128), BF))(got)
    back = jnp.concatenate([left.astype(F32), back[:, : COLS - SHIFT]], axis=1)
    grad_x = (g.astype(F32) + back).astype(BF)[None]
    gathered = lax.all_to_all(whole, FIRST, 0, 0, tiled=True)
    w, wb, p, pb, ns, nb, table = unpack(gathered)
    return (grad_x, w, wb[0], p, pb[0], ns[0], nb[0], table)


def solution(mesh):
    fine = Mesh(mesh.devices.reshape(8, 4, 2, 2, 4), ("y", "zl", "c", "zh", "x"))
    tiles = P("y", ROW, COL, None)
    return jax.shard_map(
        on_device,
        mesh=fine,
        in_specs=(tiles, tiles, P(ROW, COL), P(), P(), P(), P(), P(), P(), P()),
        out_specs=(tiles, P(), P(), P(), P(), P(), P(), P()),
        check_vma=False,
    )
```

```python
import jax
import jax.numpy as jnp
from jax import lax
from jax.experimental import pallas as pl
from jax.experimental.pallas import tpu as pltpu
from jax.sharding import Mesh, PartitionSpec as P

WIN = 8
SHIFT = 4
TOK = 64
HEADS = 6
CHAN = 192
DIM = 32
ROWS = 16
COLS = 32
TABLE = 225
OFF = 256
CHUNKS = 32
PACK = 24
BF = jnp.bfloat16
F32 = jnp.float32
HIGH = lax.Precision.HIGHEST

FIRST = ("y", "x")
SECOND = ("zl", "zh")
ROW = ("zl", "c")
COL = ("zh", "x")


def nn(a, b, precision=None):
    return lax.dot_general(a, b, (((1,), (0,)), ((), ())), precision=precision, preferred_element_type=F32)


def nt(a, b, precision=None):
    return lax.dot_general(a, b, (((1,), (1,)), ((), ())), precision=precision, preferred_element_type=F32)


def tn(a, b, precision=None):
    return lax.dot_general(a, b, (((0,), (0,)), ((), ())), precision=precision, preferred_element_type=F32)


def iota(shape, dim):
    return lax.broadcasted_iota(jnp.int32, shape, dim)


def split(a):
    high = a.astype(BF)
    return high, (a - high.astype(F32)).astype(BF)


def spread_pair():
    source, lane = iota((128, 256), 0), iota((128, 256), 1)
    head, a = source // TOK, source % TOK
    return (lane == 128 * head + 127 - (16 * (a // WIN) + a % WIN)).astype(BF)


def squeeze_pair():
    source, lane = iota((256, 128), 0), iota((256, 128), 1)
    head, a = lane // TOK, lane % TOK
    return (source == 128 * head + 16 * (a // WIN) + a % WIN).astype(F32)


def offset_sums(spread):
    blank = jnp.zeros((WIN, 128), F32)
    total = jnp.zeros((WIN, OFF), F32)
    for i in range(WIN):
        wide = jnp.concatenate([spread[WIN * i : WIN * i + WIN], blank], axis=1)
        total += pltpu.roll(wide, 16 * i, 1) if i else wide
    return jnp.sum(pltpu.roll(total, 0, 1, stride=1, stride_axis=0), 0, keepdims=True)


def prepare_kernel(pos_ref, table_ref, ls_ref, lb_ref, qb_ref, bias_ref, perm_ref, rows_ref):
    rows_ref[0, 0:CHAN] = ls_ref[...]
    rows_ref[1, 0:CHAN] = lb_ref[...]
    rows_ref[2, :] = qb_ref[...]
    pos = pos_ref[...]
    both = jnp.concatenate([pos, jnp.ones_like(pos)], axis=1).astype(F32).astype(BF)
    spread = nn(both, spread_pair())
    count = offset_sums(spread[:, 128:256])
    entry_ahead = offset_sums(spread[:, 0:128])
    back = pos.astype(F32).T
    back = jnp.concatenate([back, back], axis=1).astype(BF)
    entry_back = offset_sums(nn(back, spread_pair())[:, 0:128])

    def entry(total):
        whole = jnp.floor(total / jnp.maximum(count, 1.0) + 0.5).astype(jnp.int32)
        return jnp.where(count > 0.5, whole, -1)

    t = iota((OFF, OFF), 0)
    perm_ref[...] = (t == entry(entry_back)).astype(BF)
    perm_ahead = (iota((TABLE, OFF), 0) == entry(entry_ahead)).astype(F32)
    by_offset = nn(table_ref[...], perm_ahead, HIGH)
    squeeze = squeeze_pair()
    for pair in range(HEADS // 2):
        halves = []
        for h in (2 * pair, 2 * pair + 1):
            line = jnp.broadcast_to(by_offset[h : h + 1], (WIN, OFF))
            line = pltpu.roll(line, 129, 1, stride=1, stride_axis=0)
            shifts = [line] + [pltpu.roll(line, 16 * i, 1) for i in range(1, WIN)]
            halves.append(jnp.concatenate([a[:, 0:128] for a in shifts], axis=0))
        bias_ref[:, 128 * pair : 128 * pair + 128] = nn(
            jnp.concatenate(halves, axis=1), squeeze, HIGH
        )


def halo_kernel(x_ref, g_ref, row_ref, corner_ref):
    for i, ref in enumerate((x_ref, g_ref)):
        tile = ref[0:SHIFT]
        row_ref[i] = tile
        corner_ref[i] = tile[:, 0:SHIFT]


def main_kernel(
    x_ref,
    g_ref,
    row_ref,
    col_ref,
    corner_ref,
    ids_ref,
    w_ref,
    wp_ref,
    bias_ref,
    perm_ref,
    rows_ref,
    core_ref,
    ds_ref,
    edge_ref,
    mine_ref,
    other_ref,
    pack_ref,
    ext_ref,
    xhat_ref,
    rstd_ref,
    normed_ref,
    grad_ref,
    q_ref,
    k_ref,
    v_ref,
    da_ref,
    attn_ref,
    dq_ref,
    dk_ref,
    dv_ref,
):
    scale = DIM ** (-0.5)

    def windowed(tile_ref, which):
        ext_ref[0:ROWS, 0:COLS, :] = tile_ref[...].astype(F32)
        ext_ref[ROWS : ROWS + SHIFT, 0:COLS, :] = row_ref[which].astype(F32)
        ext_ref[0:ROWS, COLS : COLS + SHIFT, :] = col_ref[which].astype(F32)
        ext_ref[ROWS : ROWS + SHIFT, COLS : COLS + SHIFT, :] = corner_ref[which].astype(F32)
        pieces = []
        for wr in range(ROWS // WIN):
            for wc in range(COLS // WIN):
                r, c = WIN * wr + SHIFT, WIN * wc + SHIFT
                pieces.append(ext_ref[r : r + WIN, c : c + WIN, :].reshape(TOK, CHAN))
        return jnp.concatenate(pieces, axis=0)

    grad = windowed(g_ref, 1)
    grad_ref[...] = grad.astype(BF)
    grad_proj_bias = jnp.sum(grad, 0, keepdims=True)
    x = windowed(x_ref, 0)
    mean = jnp.sum(x, -1, keepdims=True) * (1.0 / CHAN)
    centered = x - mean
    rstd = lax.rsqrt(jnp.sum(centered * centered, -1, keepdims=True) * (1.0 / CHAN) + 1e-05)
    xhat = centered * rstd
    xhat_ref[...] = xhat
    rstd_ref[...] = rstd
    ls, lb, qb = rows_ref[0:1, 0:CHAN], rows_ref[1:2, 0:CHAN], rows_ref[2:3, :]
    normed = (xhat * ls + lb).astype(BF)
    normed_ref[...] = normed
    w = w_ref[...]
    w_q, w_k, w_v = w[:, 0:CHAN], w[:, CHAN : 2 * CHAN], w[:, 2 * CHAN : 3 * CHAN]
    q_ref[...] = ((nn(normed, w_q) + qb[:, 0:CHAN]) * scale).astype(BF)
    k_ref[...] = (nn(normed, w_k) + qb[:, CHAN : 2 * CHAN]).astype(BF)
    v_ref[...] = (nn(normed, w_v) + qb[:, 2 * CHAN : 3 * CHAN]).astype(BF)
    da_ref[...] = nt(grad_ref[...], wp_ref[...]).astype(BF)

    token, tile_row = iota((8 * TOK, ROWS), 0), iota((8 * TOK, ROWS), 1)
    window, inside = token // TOK, token % TOK
    pick_row = (tile_row == WIN * (window // 4) + inside // WIN).astype(BF)
    spread_ids = nn(pick_row, ids_ref[...].astype(F32).astype(BF))
    token, tile_col = iota((8 * TOK, COLS), 0), iota((8 * TOK, COLS), 1)
    window, inside = token // TOK, token % TOK
    pick_col = tile_col == WIN * (window % 4) + inside % WIN
    ids = jnp.sum(jnp.where(pick_col, spread_ids, 0.0), -1, keepdims=True)
    region = (ids == iota((8 * TOK, 16), 1).astype(F32)).astype(BF)

    head_of = iota((TOK, CHAN), 1) // DIM

    def by_head(a):
        zero = jnp.zeros_like(a)
        return jnp.concatenate([jnp.where(head_of == h, a, zero) for h in range(HEADS)], axis=0)

    def own_head(a):
        total = jnp.where(head_of == 0, a[0:TOK], 0.0)
        for h in range(1, HEADS):
            total = jnp.where(head_of == h, a[TOK * h : TOK * h + TOK], total)
        return total

    d_sum = jnp.zeros((TOK, HEADS * TOK), F32)
    for win in range(8):
        s = slice(TOK * win, TOK * win + TOK)
        q_heads = by_head(q_ref[s])
        key = k_ref[s]
        value = v_ref[s]
        apart = nt(region[s], jnp.concatenate([region[s]] * 2, axis=0)) * 100.0 - 100.0
        scores = nt(key, q_heads) + bias_ref[...] + jnp.concatenate([apart] * 3, axis=1)
        top = jnp.max(scores, 0, keepdims=True)
        e = jnp.exp(scores - top)
        p = e * (1.0 / jnp.sum(e, 0, keepdims=True))
        pb = p.astype(BF)
        attn_ref[s] = own_head(tn(pb, value)).astype(BF)
        da_heads = by_head(da_ref[s])
        d_p = nt(value, da_heads)
        dv_ref[s] = nn(pb, da_heads).astype(BF)
        d_s = p * (d_p - jnp.sum(d_p * p, 0, keepdims=True))
        d_sum += d_s
        d_sb = d_s.astype(BF)
        dq_ref[s] = (own_head(tn(d_sb, key)) * scale).astype(BF)
        dk_ref[s] = nn(d_sb, q_heads).astype(BF)

    parts = [a for pair in range(3) for a in split(d_sum[:, 128 * pair : 128 * pair + 128])]
    spread = nn(jnp.concatenate(parts, axis=0), spread_pair())
    lines = []
    for pair in range(3):
        both = spread[128 * pair : 128 * pair + TOK] + spread[128 * pair + TOK : 128 * pair + 128]
        lines += [offset_sums(both[:, 0:128]), offset_sums(both[:, 128:256])]
    lines = jnp.concatenate(lines + [jnp.zeros((2, OFF), F32)], axis=0)
    high, low = split(lines)
    by_entry = nt(jnp.concatenate([high, low], axis=0), perm_ref[...])
    by_entry = by_entry[0:8] + by_entry[8:16]

    dq, dk, dv = dq_ref[...], dk_ref[...], dv_ref[...]
    d_normed = nt(dq, w_q) + nt(dk, w_k) + nt(dv, w_v)
    xhat = xhat_ref[...]
    norm_scale = jnp.sum(d_normed * xhat, 0, keepdims=True)
    norm_bias = jnp.sum(d_normed, 0, keepdims=True)
    d_hat = d_normed * ls
    mean_hat = jnp.sum(d_hat, -1, keepdims=True) * (1.0 / CHAN)
    mean_mix = jnp.sum(d_hat * xhat, -1, keepdims=True) * (1.0 / CHAN)
    d_shifted = rstd_ref[...] * (d_hat - mean_hat - xhat * mean_mix)
    for win in range(8):
        wr, wc = win // 4, win % 4
        block = d_shifted[TOK * win : TOK * win + TOK].reshape(WIN, WIN, CHAN)
        ds_ref[WIN * wr : WIN * wr + WIN, WIN * wc : WIN * wc + WIN, :] = block
    edge_ref[...] = ds_ref[ROWS - SHIFT : ROWS].astype(BF)

    normed = normed_ref[...].T
    weights = jnp.concatenate(
        [nn(normed, dq), nn(normed, dk), nn(normed, dv), tn(attn_ref[...], grad_ref[...])], axis=1
    )
    sums = [jnp.sum(a.astype(F32), 0, keepdims=True) for a in (dq, dk, dv)] + [grad_proj_bias]
    small = jnp.concatenate(
        [
            jnp.concatenate(sums, axis=1),
            jnp.concatenate([norm_scale, norm_bias, jnp.zeros((1, 2 * CHAN), F32)], axis=1),
            jnp.concatenate([by_entry[0:1], by_entry[1:2], by_entry[2:3]], axis=1),
            jnp.concatenate([by_entry[3:4], by_entry[4:5], by_entry[5:6]], axis=1),
        ],
        axis=0,
    )
    high = small.astype(BF).astype(F32)
    small = jnp.concatenate([high, small - high], axis=0)
    packed = jnp.concatenate([weights, small], axis=0)
    for chunk in range(50):
        tiles = []
        for tile in range(3 * chunk, 3 * chunk + 3):
            r, c = tile // 6, tile % 6
            tiles.append(packed[8 * r : 8 * r + 8, 128 * c : 128 * c + 128])
        pack_ref[chunk // 25, chunk % 25] = jnp.concatenate(tiles, axis=0).astype(BF)
    pack_ref[:, 25:CHUNKS] = jnp.zeros((2, CHUNKS - 25, PACK, 128), BF)
    core = core_ref[0]
    mine_ref[...] = pack_ref[core]
    other_ref[...] = pack_ref[1 - core]


def add_up(ref, count):
    total = ref[0].astype(F32)
    for i in range(1, count):
        total += ref[i].astype(F32)
    return total


def sum_kernel(got_ref, out_ref):
    total = add_up(got_ref, got_ref.shape[0]).astype(BF)
    for i in range(out_ref.shape[0]):
        out_ref[i] = total


def pair_kernel(mine_ref, got_ref, out_ref):
    out_ref[...] = (mine_ref[...].astype(F32) + got_ref[...].astype(F32)).astype(BF)


def unpack_kernel(
    mine_ref, got_ref, core_ref, w_ref, wb_ref, p_ref, pb_ref, ns_ref, nb_ref, table_ref, half_ref, all_ref
):
    core = core_ref[0]
    half_ref[core] = mine_ref[...]
    half_ref[1 - core] = got_ref[...]
    for chunk in range(50):
        tiles = half_ref[chunk // 25, chunk % 25].astype(F32)
        for tile in range(3 * chunk, 3 * chunk + 3):
            r, c, part = tile // 6, tile % 6, 8 * (tile % 3)
            all_ref[8 * r : 8 * r + 8, 128 * c : 128 * c + 128] = tiles[part : part + 8]
    w_ref[...] = all_ref[0:CHAN, 0 : 3 * CHAN]
    p_ref[...] = all_ref[0:CHAN, 3 * CHAN : 4 * CHAN]
    small = all_ref[CHAN : CHAN + 4, :] + all_ref[CHAN + 4 : CHAN + 8, :]
    wb_ref[...] = small[0, 0 : 3 * CHAN]
    pb_ref[...] = small[0, 3 * CHAN : 4 * CHAN]
    ns_ref[...] = small[1, 0:CHAN]
    nb_ref[...] = small[1, CHAN : 2 * CHAN]
    for h in range(HEADS):
        place = OFF * (h % 3)
        table_ref[h : h + 1, :] = small[2 + h // 3 : 3 + h // 3, place : place + TABLE]


def kernel_call(kernel, out_shape, scratch=(), flops=10**7, **specs):
    return pl.pallas_call(
        kernel,
        out_shape=out_shape,
        scratch_shapes=scratch,
        **specs,
        cost_estimate=pl.CostEstimate(flops=flops, bytes_accessed=10**6, transcendentals=0),
        compiler_params=pltpu.CompilerParams(vmem_limit_bytes=40 * 2**20),
    )


def shape(dims, kind=F32):
    return jax.ShapeDtypeStruct(dims, kind)


def moved(block, axes, distance):
    sizes = [lax.axis_size(a) for a in axes]
    count = sizes[0] * sizes[1]
    return lax.ppermute(block, axes, [((i - distance) % count, i) for i in range(count)])


def moved_corner(block):
    pairs = [
        (8 * ((r + 1) % 8) + (c + 1) % 8, 8 * r + c) for r in range(8) for c in range(8)
    ]
    return lax.ppermute(block, ROW + COL, pairs)


SMALL = pl.BlockSpec(memory_space=pltpu.SMEM)
WHOLE = pl.BlockSpec(memory_space=pltpu.VMEM)


def prepare(position_index, bias_table, ls, lb, qb):
    return kernel_call(
        prepare_kernel,
        (shape((TOK, HEADS * TOK)), shape((OFF, OFF), BF), shape((8, 3 * CHAN))),
    )(position_index, bias_table.T, ls, lb, qb)


def halos(x, g):
    return kernel_call(
        halo_kernel,
        (
            shape((2, SHIFT, COLS, CHAN), BF),
            shape((2, SHIFT, SHIFT, CHAN), BF),
        ),
    )(x, g)


def main(*args):
    tokens = 8 * TOK
    return kernel_call(
        main_kernel,
        (
            shape((ROWS, COLS, CHAN)),
            shape((SHIFT, COLS, CHAN), BF),
            shape((CHUNKS, PACK, 128), BF),
            shape((CHUNKS, PACK, 128), BF),
        ),
        [
            pltpu.VMEM((2, CHUNKS, PACK, 128), BF),
            pltpu.VMEM((ROWS + 8, COLS + 8, CHAN), F32),
            pltpu.VMEM((tokens, CHAN), F32),
            pltpu.VMEM((tokens, 1), F32),
        ]
        + [pltpu.VMEM((tokens, CHAN), BF)] * 10,
        flops=10**9,
        in_specs=[WHOLE] * (len(args) - 1) + [SMALL],
    )(*args)


def pair_sum(mine, got):
    return kernel_call(pair_kernel, shape(mine.shape, BF))(mine, got)


def chunk_sum(got, copies):
    return kernel_call(sum_kernel, shape((copies,) + got.shape[1:], BF))(got)


def unpack(mine, got, core):
    return kernel_call(
        unpack_kernel,
        (
            shape((CHAN, 3 * CHAN)),
            shape((3 * CHAN,)),
            shape((CHAN, CHAN)),
            shape((CHAN,)),
            shape((CHAN,)),
            shape((CHAN,)),
            shape((HEADS, TABLE)),
        ),
        [pltpu.VMEM((2, CHUNKS, PACK, 128), BF), pltpu.VMEM((CHAN + 8, 4 * CHAN), F32)],
        in_specs=[WHOLE, WHOLE, SMALL],
    )(mine, got, core)


def on_device(
    block_input,
    grad_out,
    region_ids,
    layernorm_scale,
    layernorm_bias,
    qkv_weight,
    qkv_bias,
    proj_weight,
    bias_table,
    position_index,
):
    x, g = block_input[0], grad_out[0]
    core = lax.axis_index("c").astype(jnp.int32)[None]
    col = moved(jnp.stack([x[:, :SHIFT], g[:, :SHIFT]]), COL, -1)
    row, corner = halos(x, g)
    row, corner = moved(row, ROW, -1), moved_corner(corner)
    bias, perm, rows = prepare(
        position_index, bias_table, layernorm_scale, layernorm_bias, qkv_bias
    )
    d_shifted, edge, mine, other = main(
        x, g, row, col, corner, region_ids, qkv_weight, proj_weight, bias, perm, rows, core
    )
    half = pair_sum(mine, lax.ppermute(other, "c", [(0, 1), (1, 0)]))
    above = moved(edge, ROW, 1)
    got = lax.all_to_all(half, FIRST, 0, 0, tiled=True)
    part = chunk_sum(got, 8)
    got = lax.all_to_all(part, SECOND, 0, 0, tiled=True)
    whole = chunk_sum(got, CHUNKS)
    back = jnp.concatenate([above.astype(F32), d_shifted[: ROWS - SHIFT]], axis=0)
    left = moved(back[:, COLS - SHIFT :].astype(BF), COL, 1)
    back = jnp.concatenate([left.astype(F32), back[:, : COLS - SHIFT]], axis=1)
    grad_x = (g.astype(F32) + back).astype(BF)[None]
    gathered = lax.all_to_all(whole, FIRST, 0, 0, tiled=True)
    other = lax.ppermute(gathered, "c", [(0, 1), (1, 0)])
    w, wb, p, pb, ns, nb, table = unpack(gathered, other, core)
    return (grad_x, w, wb, p, pb, ns, nb, table.T)


def solution(mesh):
    fine = Mesh(mesh.devices.reshape(8, 4, 2, 2, 4), ("y", "zl", "c", "zh", "x"))
    tiles = P("y", ROW, COL, None)
    return jax.shard_map(
        on_device,
        mesh=fine,
        in_specs=(tiles, tiles, P(ROW, COL), P(), P(), P(), P(), P(), P(), P()),
        out_specs=(tiles, P(), P(), P(), P(), P(), P(), P()),
        check_vma=False,
    )
```

```python
import jax
import jax.numpy as jnp
from jax import lax
from jax.experimental import pallas as pl
from jax.experimental.pallas import tpu as pltpu
from jax.sharding import Mesh, PartitionSpec as P

WIN = 8
SHIFT = 4
TOK = 64
HEADS = 6
CHAN = 192
DIM = 32
ROWS = 16
COLS = 32
TABLE = 225
OFF = 256
CHUNKS = 32
PACK = 24
BF = jnp.bfloat16
F32 = jnp.float32
HIGH = lax.Precision.HIGHEST

FIRST = ("y", "x")
SECOND = ("zl", "zh")
ROW = ("zl", "c")
COL = ("zh", "x")


def nn(a, b, precision=None):
    return lax.dot_general(a, b, (((1,), (0,)), ((), ())), precision=precision, preferred_element_type=F32)


def nt(a, b, precision=None):
    return lax.dot_general(a, b, (((1,), (1,)), ((), ())), precision=precision, preferred_element_type=F32)


def tn(a, b, precision=None):
    return lax.dot_general(a, b, (((0,), (0,)), ((), ())), precision=precision, preferred_element_type=F32)


def iota(shape, dim):
    return lax.broadcasted_iota(jnp.int32, shape, dim)


def split(a):
    high = a.astype(BF)
    return high, (a - high.astype(F32)).astype(BF)


def spread_pair():
    source, lane = iota((128, 256), 0), iota((128, 256), 1)
    head, a = source // TOK, source % TOK
    return (lane == 128 * head + 127 - (16 * (a // WIN) + a % WIN)).astype(BF)


def squeeze_pair():
    source, lane = iota((256, 128), 0), iota((256, 128), 1)
    head, a = lane // TOK, lane % TOK
    return (source == 128 * head + 16 * (a // WIN) + a % WIN).astype(F32)


def offset_sums(spread):
    blank = jnp.zeros((WIN, 128), F32)
    total = jnp.zeros((WIN, OFF), F32)
    for i in range(WIN):
        wide = jnp.concatenate([spread[WIN * i : WIN * i + WIN], blank], axis=1)
        total += pltpu.roll(wide, 16 * i, 1) if i else wide
    return jnp.sum(pltpu.roll(total, 0, 1, stride=1, stride_axis=0), 0, keepdims=True)


def prepare_kernel(
    pos_ref,
    table_ref,
    ids_ref,
    w_ref,
    ls_ref,
    lb_ref,
    qb_ref,
    bias_ref,
    perm_ref,
    apart_ref,
    parts_ref,
    rows_ref,
):
    rows_ref[0, 0:CHAN] = ls_ref[...]
    rows_ref[1, 0:CHAN] = lb_ref[...]
    rows_ref[2, :] = qb_ref[...]
    w = w_ref[...]
    for i in range(3):
        parts_ref[i] = w[:, CHAN * i : CHAN * i + CHAN]

    token, tile_row = iota((8 * TOK, ROWS), 0), iota((8 * TOK, ROWS), 1)
    window, inside = token // TOK, token % TOK
    pick_row = (tile_row == WIN * (window // 4) + inside // WIN).astype(BF)
    spread_ids = nn(pick_row, ids_ref[...].astype(F32).astype(BF))
    token, tile_col = iota((8 * TOK, COLS), 0), iota((8 * TOK, COLS), 1)
    window, inside = token // TOK, token % TOK
    pick_col = tile_col == WIN * (window % 4) + inside % WIN
    ids = jnp.sum(jnp.where(pick_col, spread_ids, 0.0), -1, keepdims=True)
    region = (ids == iota((8 * TOK, 16), 1).astype(F32)).astype(BF)
    for win in range(8):
        own = region[TOK * win : TOK * win + TOK]
        apart_ref[win] = nt(own, jnp.concatenate([own, own], axis=0)) * 100.0 - 100.0

    pos = pos_ref[...]
    both = jnp.concatenate([pos, jnp.ones_like(pos)], axis=1).astype(F32).astype(BF)
    spread = nn(both, spread_pair())
    count = offset_sums(spread[:, 128:256])
    entry_ahead = offset_sums(spread[:, 0:128])
    back = pos.astype(F32).T
    back = jnp.concatenate([back, back], axis=1).astype(BF)
    entry_back = offset_sums(nn(back, spread_pair())[:, 0:128])

    def entry(total):
        whole = jnp.floor(total / jnp.maximum(count, 1.0) + 0.5).astype(jnp.int32)
        return jnp.where(count > 0.5, whole, -1)

    t = iota((OFF, OFF), 0)
    perm_ref[...] = (t == entry(entry_back)).astype(BF)
    perm_ahead = (iota((TABLE, OFF), 0) == entry(entry_ahead)).astype(F32)
    by_offset = nn(table_ref[...], perm_ahead, HIGH)
    squeeze = squeeze_pair()
    for pair in range(HEADS // 2):
        halves = []
        for h in (2 * pair, 2 * pair + 1):
            line = jnp.broadcast_to(by_offset[h : h + 1], (WIN, OFF))
            line = pltpu.roll(line, 129, 1, stride=1, stride_axis=0)
            shifts = [line] + [pltpu.roll(line, 16 * i, 1) for i in range(1, WIN)]
            halves.append(jnp.concatenate([a[:, 0:128] for a in shifts], axis=0))
        bias_ref[:, 128 * pair : 128 * pair + 128] = nn(
            jnp.concatenate(halves, axis=1), squeeze, HIGH
        )


def halo_kernel(x_ref, g_ref, row_ref, corner_ref):
    for i, ref in enumerate((x_ref, g_ref)):
        tile = ref[0:SHIFT]
        row_ref[i] = tile
        corner_ref[i] = tile[:, 0:SHIFT]


def main_kernel(
    x_ref,
    g_ref,
    row_ref,
    col_ref,
    corner_ref,
    parts_ref,
    wp_ref,
    bias_ref,
    perm_ref,
    apart_ref,
    rows_ref,
    core_ref,
    ds_ref,
    edge_ref,
    mine_ref,
    other_ref,
    pack_ref,
    ext_ref,
    xhat_ref,
    rstd_ref,
    normed_ref,
    grad_ref,
    q_ref,
    k_ref,
    v_ref,
    da_ref,
    attn_ref,
    dq_ref,
    dk_ref,
    dv_ref,
    qh_ref,
    dah_ref,
    p_ref,
    dp_ref,
    pb_ref,
    dsb_ref,
):
    scale = DIM ** (-0.5)

    def windowed(tile_ref, which):
        ext_ref[0:ROWS, 0:COLS, :] = tile_ref[...].astype(F32)
        ext_ref[ROWS : ROWS + SHIFT, 0:COLS, :] = row_ref[which].astype(F32)
        ext_ref[0:ROWS, COLS : COLS + SHIFT, :] = col_ref[which].astype(F32)
        ext_ref[ROWS : ROWS + SHIFT, COLS : COLS + SHIFT, :] = corner_ref[which].astype(F32)
        pieces = []
        for wr in range(ROWS // WIN):
            for wc in range(COLS // WIN):
                r, c = WIN * wr + SHIFT, WIN * wc + SHIFT
                pieces.append(ext_ref[r : r + WIN, c : c + WIN, :].reshape(TOK, CHAN))
        return jnp.concatenate(pieces, axis=0)

    grad = windowed(g_ref, 1)
    grad_ref[...] = grad.astype(BF)
    grad_proj_bias = jnp.sum(grad, 0, keepdims=True)
    x = windowed(x_ref, 0)
    mean = jnp.sum(x, -1, keepdims=True) * (1.0 / CHAN)
    centered = x - mean
    rstd = lax.rsqrt(jnp.sum(centered * centered, -1, keepdims=True) * (1.0 / CHAN) + 1e-05)
    xhat = centered * rstd
    xhat_ref[...] = xhat
    rstd_ref[...] = rstd
    ls, lb, qb = rows_ref[0:1, 0:CHAN], rows_ref[1:2, 0:CHAN], rows_ref[2:3, :]
    normed = (xhat * ls + lb).astype(BF)
    normed_ref[...] = normed
    w_q, w_k, w_v = parts_ref[0], parts_ref[1], parts_ref[2]
    q_ref[...] = ((nn(normed, w_q) + qb[:, 0:CHAN]) * scale).astype(BF)
    k_ref[...] = (nn(normed, w_k) + qb[:, CHAN : 2 * CHAN]).astype(BF)
    v_ref[...] = (nn(normed, w_v) + qb[:, 2 * CHAN : 3 * CHAN]).astype(BF)
    da_ref[...] = nt(grad_ref[...], wp_ref[...]).astype(BF)

    head_of = iota((TOK, CHAN), 1) // DIM

    def by_head(a):
        zero = jnp.zeros_like(a)
        return jnp.concatenate([jnp.where(head_of == h, a, zero) for h in range(HEADS)], axis=0)

    def own_head(a):
        total = jnp.where(head_of == 0, a[0:TOK], 0.0)
        for h in range(1, HEADS):
            total = jnp.where(head_of == h, a[TOK * h : TOK * h + TOK], total)
        return total

    windows = [slice(TOK * win, TOK * win + TOK) for win in range(8)]
    for win, s in enumerate(windows):
        qh_ref[win] = by_head(q_ref[s])
        dah_ref[win] = by_head(da_ref[s])
    for win, s in enumerate(windows):
        apart = jnp.concatenate([apart_ref[win]] * 3, axis=1)
        p_ref[win] = nt(k_ref[s], qh_ref[win]) + bias_ref[...] + apart
        dp_ref[win] = nt(v_ref[s], dah_ref[win])
    d_sum = jnp.zeros((TOK, HEADS * TOK), F32)
    for win in range(8):
        scores = p_ref[win]
        e = jnp.exp(scores - jnp.max(scores, 0, keepdims=True))
        p = e * (1.0 / jnp.sum(e, 0, keepdims=True))
        pb_ref[win] = p.astype(BF)
        d_p = dp_ref[win]
        d_s = p * (d_p - jnp.sum(d_p * p, 0, keepdims=True))
        d_sum += d_s
        dsb_ref[win] = d_s.astype(BF)
    for win, s in enumerate(windows):
        attn_ref[s] = own_head(tn(pb_ref[win], v_ref[s])).astype(BF)
        dv_ref[s] = nn(pb_ref[win], dah_ref[win]).astype(BF)
        dq_ref[s] = (own_head(tn(dsb_ref[win], k_ref[s])) * scale).astype(BF)
        dk_ref[s] = nn(dsb_ref[win], qh_ref[win]).astype(BF)

    parts = [a for pair in range(3) for a in split(d_sum[:, 128 * pair : 128 * pair + 128])]
    spread = nn(jnp.concatenate(parts, axis=0), spread_pair())
    lines = []
    for pair in range(3):
        both = spread[128 * pair : 128 * pair + TOK] + spread[128 * pair + TOK : 128 * pair + 128]
        lines += [offset_sums(both[:, 0:128]), offset_sums(both[:, 128:256])]
    lines = jnp.concatenate(lines + [jnp.zeros((2, OFF), F32)], axis=0)
    high, low = split(lines)
    by_entry = nt(jnp.concatenate([high, low], axis=0), perm_ref[...])
    by_entry = by_entry[0:8] + by_entry[8:16]

    dq, dk, dv = dq_ref[...], dk_ref[...], dv_ref[...]
    d_normed = nt(dq, w_q) + nt(dk, w_k) + nt(dv, w_v)
    xhat = xhat_ref[...]
    norm_scale = jnp.sum(d_normed * xhat, 0, keepdims=True)
    norm_bias = jnp.sum(d_normed, 0, keepdims=True)
    d_hat = d_normed * ls
    mean_hat = jnp.sum(d_hat, -1, keepdims=True) * (1.0 / CHAN)
    mean_mix = jnp.sum(d_hat * xhat, -1, keepdims=True) * (1.0 / CHAN)
    d_shifted = rstd_ref[...] * (d_hat - mean_hat - xhat * mean_mix)
    for win in range(8):
        wr, wc = win // 4, win % 4
        block = d_shifted[TOK * win : TOK * win + TOK].reshape(WIN, WIN, CHAN)
        ds_ref[WIN * wr : WIN * wr + WIN, WIN * wc : WIN * wc + WIN, :] = block
    edge_ref[...] = ds_ref[ROWS - SHIFT : ROWS].astype(BF)

    normed = normed_ref[...].T
    weights = jnp.concatenate(
        [nn(normed, dq), nn(normed, dk), nn(normed, dv), tn(attn_ref[...], grad_ref[...])], axis=1
    )
    sums = [jnp.sum(a.astype(F32), 0, keepdims=True) for a in (dq, dk, dv)] + [grad_proj_bias]
    small = jnp.concatenate(
        [
            jnp.concatenate(sums, axis=1),
            jnp.concatenate([norm_scale, norm_bias, jnp.zeros((1, 2 * CHAN), F32)], axis=1),
            jnp.concatenate([by_entry[0:1], by_entry[1:2], by_entry[2:3]], axis=1),
            jnp.concatenate([by_entry[3:4], by_entry[4:5], by_entry[5:6]], axis=1),
        ],
        axis=0,
    )
    high = small.astype(BF).astype(F32)
    small = jnp.concatenate([high, small - high], axis=0)
    packed = jnp.concatenate([weights, small], axis=0)
    for chunk in range(50):
        tiles = []
        for tile in range(3 * chunk, 3 * chunk + 3):
            r, c = tile // 6, tile % 6
            tiles.append(packed[8 * r : 8 * r + 8, 128 * c : 128 * c + 128])
        pack_ref[chunk // 25, chunk % 25] = jnp.concatenate(tiles, axis=0).astype(BF)
    pack_ref[:, 25:CHUNKS] = jnp.zeros((2, CHUNKS - 25, PACK, 128), BF)
    core = core_ref[0]
    mine_ref[...] = pack_ref[core]
    other_ref[...] = pack_ref[1 - core]


def add_up(ref, count):
    total = ref[0].astype(F32)
    for i in range(1, count):
        total += ref[i].astype(F32)
    return total


def sum_kernel(got_ref, after_ref, out_ref):
    total = add_up(got_ref, got_ref.shape[0]).astype(BF)
    for i in range(out_ref.shape[0]):
        out_ref[i] = total


def sum_edge_kernel(got_ref, above_ref, ds_ref, out_ref, edge_ref):
    total = add_up(got_ref, got_ref.shape[0]).astype(BF)
    for i in range(out_ref.shape[0]):
        out_ref[i] = total
    edge_ref[0:SHIFT] = above_ref[:, COLS - SHIFT : COLS]
    edge_ref[SHIFT:ROWS] = ds_ref[0 : ROWS - SHIFT, COLS - SHIFT : COLS].astype(BF)


def pair_kernel(mine_ref, got_ref, out_ref):
    out_ref[...] = (mine_ref[...].astype(F32) + got_ref[...].astype(F32)).astype(BF)


def unpack_kernel(
    mine_ref, got_ref, core_ref, w_ref, wb_ref, p_ref, pb_ref, ns_ref, nb_ref, table_ref, half_ref, all_ref
):
    core = core_ref[0]
    half_ref[core] = mine_ref[...]
    half_ref[1 - core] = got_ref[...]
    for chunk in range(50):
        tiles = half_ref[chunk // 25, chunk % 25].astype(F32)
        for tile in range(3 * chunk, 3 * chunk + 3):
            r, c, part = tile // 6, tile % 6, 8 * (tile % 3)
            all_ref[8 * r : 8 * r + 8, 128 * c : 128 * c + 128] = tiles[part : part + 8]
    w_ref[...] = all_ref[0:CHAN, 0 : 3 * CHAN]
    p_ref[...] = all_ref[0:CHAN, 3 * CHAN : 4 * CHAN]
    small = all_ref[CHAN : CHAN + 4, :] + all_ref[CHAN + 4 : CHAN + 8, :]
    wb_ref[...] = small[0, 0 : 3 * CHAN]
    pb_ref[...] = small[0, 3 * CHAN : 4 * CHAN]
    ns_ref[...] = small[1, 0:CHAN]
    nb_ref[...] = small[1, CHAN : 2 * CHAN]
    for h in range(HEADS):
        place = OFF * (h % 3)
        table_ref[h : h + 1, :] = small[2 + h // 3 : 3 + h // 3, place : place + TABLE]


def kernel_call(kernel, out_shape, scratch=(), flops=10**7, **specs):
    return pl.pallas_call(
        kernel,
        out_shape=out_shape,
        scratch_shapes=scratch,
        **specs,
        cost_estimate=pl.CostEstimate(flops=flops, bytes_accessed=10**6, transcendentals=0),
        compiler_params=pltpu.CompilerParams(vmem_limit_bytes=40 * 2**20),
    )


def shape(dims, kind=F32):
    return jax.ShapeDtypeStruct(dims, kind)


def moved(block, axes, distance):
    sizes = [lax.axis_size(a) for a in axes]
    count = sizes[0] * sizes[1]
    return lax.ppermute(block, axes, [((i - distance) % count, i) for i in range(count)])


def moved_corner(block):
    pairs = [
        (8 * ((r + 1) % 8) + (c + 1) % 8, 8 * r + c) for r in range(8) for c in range(8)
    ]
    return lax.ppermute(block, ROW + COL, pairs)


SMALL = pl.BlockSpec(memory_space=pltpu.SMEM)
WHOLE = pl.BlockSpec(memory_space=pltpu.VMEM)


def prepare(*args):
    return kernel_call(
        prepare_kernel,
        (
            shape((TOK, HEADS * TOK)),
            shape((OFF, OFF), BF),
            shape((8, TOK, 128)),
            shape((3, CHAN, CHAN), BF),
            shape((8, 3 * CHAN)),
        ),
    )(*args)


def halos(x, g):
    return kernel_call(
        halo_kernel,
        (
            shape((2, SHIFT, COLS, CHAN), BF),
            shape((2, SHIFT, SHIFT, CHAN), BF),
        ),
    )(x, g)


def main(*args):
    tokens = 8 * TOK
    return kernel_call(
        main_kernel,
        (
            shape((ROWS, COLS, CHAN)),
            shape((SHIFT, COLS, CHAN), BF),
            shape((CHUNKS, PACK, 128), BF),
            shape((CHUNKS, PACK, 128), BF),
        ),
        [
            pltpu.VMEM((2, CHUNKS, PACK, 128), BF),
            pltpu.VMEM((ROWS + 8, COLS + 8, CHAN), F32),
            pltpu.VMEM((tokens, CHAN), F32),
            pltpu.VMEM((tokens, 1), F32),
        ]
        + [pltpu.VMEM((tokens, CHAN), BF)] * 10
        + [pltpu.VMEM((8, HEADS * TOK, CHAN), BF)] * 2
        + [pltpu.VMEM((8, TOK, HEADS * TOK), F32)] * 2
        + [pltpu.VMEM((8, TOK, HEADS * TOK), BF)] * 2,
        flops=10**9,
        in_specs=[WHOLE] * (len(args) - 1) + [SMALL],
    )(*args)


def pair_sum(mine, got):
    return kernel_call(pair_kernel, shape(mine.shape, BF))(mine, got)


def chunk_sum(got, copies, after):
    return kernel_call(sum_kernel, shape((copies,) + got.shape[1:], BF))(got, after)


def chunk_sum_edge(got, copies, above, d_shifted):
    return kernel_call(
        sum_edge_kernel,
        (shape((copies,) + got.shape[1:], BF), shape((ROWS, SHIFT, CHAN), BF)),
    )(got, above, d_shifted)


def unpack(mine, got, core):
    return kernel_call(
        unpack_kernel,
        (
            shape((CHAN, 3 * CHAN)),
            shape((3 * CHAN,)),
            shape((CHAN, CHAN)),
            shape((CHAN,)),
            shape((CHAN,)),
            shape((CHAN,)),
            shape((HEADS, TABLE)),
        ),
        [pltpu.VMEM((2, CHUNKS, PACK, 128), BF), pltpu.VMEM((CHAN + 8, 4 * CHAN), F32)],
        in_specs=[WHOLE, WHOLE, SMALL],
    )(mine, got, core)


def on_device(
    block_input,
    grad_out,
    region_ids,
    layernorm_scale,
    layernorm_bias,
    qkv_weight,
    qkv_bias,
    proj_weight,
    bias_table,
    position_index,
):
    x, g = block_input[0], grad_out[0]
    core = lax.axis_index("c").astype(jnp.int32)[None]
    col = moved(jnp.stack([x[:, :SHIFT], g[:, :SHIFT]]), COL, -1)
    row, corner = halos(x, g)
    row, corner = moved(row, ROW, -1), moved_corner(corner)
    bias, perm, apart, parts, rows = prepare(
        position_index, bias_table.T, region_ids, qkv_weight, layernorm_scale, layernorm_bias, qkv_bias
    )
    d_shifted, edge, mine, other = main(
        x, g, row, col, corner, parts, proj_weight, bias, perm, apart, rows, core
    )
    half = pair_sum(mine, lax.ppermute(other, "c", [(0, 1), (1, 0)]))
    above = moved(edge, ROW, 1)
    got = lax.all_to_all(half, FIRST, 0, 0, tiled=True)
    part = chunk_sum(got, 8, above)
    got = lax.all_to_all(part, SECOND, 0, 0, tiled=True)
    whole, edge = chunk_sum_edge(got, CHUNKS, above, d_shifted)
    left = moved(edge, COL, 1)
    gathered = lax.all_to_all(whole, FIRST, 0, 0, tiled=True)
    back = jnp.concatenate([above.astype(F32), d_shifted[: ROWS - SHIFT]], axis=0)
    back = jnp.concatenate([left.astype(F32), back[:, : COLS - SHIFT]], axis=1)
    grad_x = (g.astype(F32) + back).astype(BF)[None]
    other = lax.ppermute(gathered, "c", [(0, 1), (1, 0)])
    w, wb, p, pb, ns, nb, table = unpack(gathered, other, core)
    return (grad_x, w, wb, p, pb, ns, nb, table.T)


def solution(mesh):
    fine = Mesh(mesh.devices.reshape(8, 4, 2, 2, 4), ("y", "zl", "c", "zh", "x"))
    tiles = P("y", ROW, COL, None)
    return jax.shard_map(
        on_device,
        mesh=fine,
        in_specs=(tiles, tiles, P(ROW, COL), P(), P(), P(), P(), P(), P(), P()),
        out_specs=(tiles, P(), P(), P(), P(), P(), P(), P()),
        check_vma=False,
    )
```

```python
import jax
import jax.numpy as jnp
from jax import lax
from jax.experimental import pallas as pl
from jax.experimental.pallas import tpu as pltpu
from jax.sharding import Mesh, PartitionSpec as P

WIN = 8
SHIFT = 4
TOK = 64
HEADS = 6
CHAN = 192
DIM = 32
ROWS = 16
COLS = 32
TABLE = 225
OFF = 256
CHUNKS = 32
PACK = 40
BF = jnp.bfloat16
F32 = jnp.float32
HIGH = lax.Precision.HIGHEST

FIRST = ("y", "x")
SECOND = ("zl", "c", "zh")
ROW = ("zl", "c")
COL = ("zh", "x")


def nn(a, b, precision=None):
    return lax.dot_general(a, b, (((1,), (0,)), ((), ())), precision=precision, preferred_element_type=F32)


def nt(a, b, precision=None):
    return lax.dot_general(a, b, (((1,), (1,)), ((), ())), precision=precision, preferred_element_type=F32)


def tn(a, b, precision=None):
    return lax.dot_general(a, b, (((0,), (0,)), ((), ())), precision=precision, preferred_element_type=F32)


def iota(shape, dim):
    return lax.broadcasted_iota(jnp.int32, shape, dim)


def split(a):
    high = a.astype(BF)
    return high, (a - high.astype(F32)).astype(BF)


def spread_pair():
    source, lane = iota((128, 256), 0), iota((128, 256), 1)
    head, a = source // TOK, source % TOK
    return (lane == 128 * head + 127 - (16 * (a // WIN) + a % WIN)).astype(BF)


def squeeze_pair():
    source, lane = iota((256, 128), 0), iota((256, 128), 1)
    head, a = lane // TOK, lane % TOK
    return (source == 128 * head + 16 * (a // WIN) + a % WIN).astype(F32)


def offset_sums(spread):
    blank = jnp.zeros((WIN, 128), F32)
    total = jnp.zeros((WIN, OFF), F32)
    for i in range(WIN):
        wide = jnp.concatenate([spread[WIN * i : WIN * i + WIN], blank], axis=1)
        total += pltpu.roll(wide, 16 * i, 1) if i else wide
    return jnp.sum(pltpu.roll(total, 0, 1, stride=1, stride_axis=0), 0, keepdims=True)


def prepare_kernel(
    pos_ref,
    table_ref,
    ids_ref,
    w_ref,
    ls_ref,
    lb_ref,
    qb_ref,
    bias_ref,
    perm_ref,
    apart_ref,
    parts_ref,
    rows_ref,
):
    rows_ref[0, 0:CHAN] = ls_ref[...]
    rows_ref[1, 0:CHAN] = lb_ref[...]
    rows_ref[2, :] = qb_ref[...]
    w = w_ref[...]
    for i in range(3):
        parts_ref[i] = w[:, CHAN * i : CHAN * i + CHAN]

    token, tile_row = iota((8 * TOK, ROWS), 0), iota((8 * TOK, ROWS), 1)
    window, inside = token // TOK, token % TOK
    pick_row = (tile_row == WIN * (window // 4) + inside // WIN).astype(BF)
    spread_ids = nn(pick_row, ids_ref[...].astype(F32).astype(BF))
    token, tile_col = iota((8 * TOK, COLS), 0), iota((8 * TOK, COLS), 1)
    window, inside = token // TOK, token % TOK
    pick_col = tile_col == WIN * (window % 4) + inside % WIN
    ids = jnp.sum(jnp.where(pick_col, spread_ids, 0.0), -1, keepdims=True)
    region = (ids == iota((8 * TOK, 16), 1).astype(F32)).astype(BF)
    for win in range(8):
        own = region[TOK * win : TOK * win + TOK]
        apart_ref[win] = nt(own, jnp.concatenate([own, own], axis=0)) * 100.0 - 100.0

    pos = pos_ref[...]
    both = jnp.concatenate([pos, jnp.ones_like(pos)], axis=1).astype(F32).astype(BF)
    spread = nn(both, spread_pair())
    count = offset_sums(spread[:, 128:256])
    entry_ahead = offset_sums(spread[:, 0:128])
    back = pos.astype(F32).T
    back = jnp.concatenate([back, back], axis=1).astype(BF)
    entry_back = offset_sums(nn(back, spread_pair())[:, 0:128])

    def entry(total):
        whole = jnp.floor(total / jnp.maximum(count, 1.0) + 0.5).astype(jnp.int32)
        return jnp.where(count > 0.5, whole, -1)

    t = iota((OFF, OFF), 0)
    perm_ref[...] = (t == entry(entry_back)).astype(BF)
    perm_ahead = (iota((TABLE, OFF), 0) == entry(entry_ahead)).astype(F32)
    by_offset = nn(table_ref[...], perm_ahead, HIGH)
    squeeze = squeeze_pair()
    for pair in range(HEADS // 2):
        halves = []
        for h in (2 * pair, 2 * pair + 1):
            line = jnp.broadcast_to(by_offset[h : h + 1], (WIN, OFF))
            line = pltpu.roll(line, 129, 1, stride=1, stride_axis=0)
            shifts = [line] + [pltpu.roll(line, 16 * i, 1) for i in range(1, WIN)]
            halves.append(jnp.concatenate([a[:, 0:128] for a in shifts], axis=0))
        bias_ref[:, 128 * pair : 128 * pair + 128] = nn(
            jnp.concatenate(halves, axis=1), squeeze, HIGH
        )


def halo_kernel(x_ref, g_ref, row_ref, corner_ref):
    for i, ref in enumerate((x_ref, g_ref)):
        tile = ref[0:SHIFT]
        row_ref[i] = tile
        corner_ref[i] = tile[:, 0:SHIFT]


def main_kernel(
    x_ref,
    g_ref,
    row_ref,
    col_ref,
    corner_ref,
    parts_ref,
    wp_ref,
    bias_ref,
    perm_ref,
    apart_ref,
    rows_ref,
    ds_ref,
    edge_ref,
    pack_ref,
    ext_ref,
    xhat_ref,
    rstd_ref,
    normed_ref,
    grad_ref,
    q_ref,
    k_ref,
    v_ref,
    da_ref,
    attn_ref,
    dq_ref,
    dk_ref,
    dv_ref,
    qh_ref,
    dah_ref,
    p_ref,
    dp_ref,
    pb_ref,
    dsb_ref,
):
    scale = DIM ** (-0.5)

    def windowed(tile_ref, which):
        ext_ref[0:ROWS, 0:COLS, :] = tile_ref[...].astype(F32)
        ext_ref[ROWS : ROWS + SHIFT, 0:COLS, :] = row_ref[which].astype(F32)
        ext_ref[0:ROWS, COLS : COLS + SHIFT, :] = col_ref[which].astype(F32)
        ext_ref[ROWS : ROWS + SHIFT, COLS : COLS + SHIFT, :] = corner_ref[which].astype(F32)
        pieces = []
        for wr in range(ROWS // WIN):
            for wc in range(COLS // WIN):
                r, c = WIN * wr + SHIFT, WIN * wc + SHIFT
                pieces.append(ext_ref[r : r + WIN, c : c + WIN, :].reshape(TOK, CHAN))
        return jnp.concatenate(pieces, axis=0)

    grad = windowed(g_ref, 1)
    grad_ref[...] = grad.astype(BF)
    grad_proj_bias = jnp.sum(grad, 0, keepdims=True)
    x = windowed(x_ref, 0)
    mean = jnp.sum(x, -1, keepdims=True) * (1.0 / CHAN)
    centered = x - mean
    rstd = lax.rsqrt(jnp.sum(centered * centered, -1, keepdims=True) * (1.0 / CHAN) + 1e-05)
    xhat = centered * rstd
    xhat_ref[...] = xhat
    rstd_ref[...] = rstd
    ls, lb, qb = rows_ref[0:1, 0:CHAN], rows_ref[1:2, 0:CHAN], rows_ref[2:3, :]
    normed = (xhat * ls + lb).astype(BF)
    normed_ref[...] = normed
    w_q, w_k, w_v = parts_ref[0], parts_ref[1], parts_ref[2]
    q_ref[...] = ((nn(normed, w_q) + qb[:, 0:CHAN]) * scale).astype(BF)
    k_ref[...] = (nn(normed, w_k) + qb[:, CHAN : 2 * CHAN]).astype(BF)
    v_ref[...] = (nn(normed, w_v) + qb[:, 2 * CHAN : 3 * CHAN]).astype(BF)
    da_ref[...] = nt(grad_ref[...], wp_ref[...]).astype(BF)

    head_of = iota((TOK, CHAN), 1) // DIM

    def by_head(a):
        zero = jnp.zeros_like(a)
        return jnp.concatenate([jnp.where(head_of == h, a, zero) for h in range(HEADS)], axis=0)

    def own_head(a):
        total = jnp.where(head_of == 0, a[0:TOK], 0.0)
        for h in range(1, HEADS):
            total = jnp.where(head_of == h, a[TOK * h : TOK * h + TOK], total)
        return total

    windows = [slice(TOK * win, TOK * win + TOK) for win in range(8)]
    for win, s in enumerate(windows):
        qh_ref[win] = by_head(q_ref[s])
        dah_ref[win] = by_head(da_ref[s])
    for win, s in enumerate(windows):
        apart = jnp.concatenate([apart_ref[win]] * 3, axis=1)
        p_ref[win] = nt(k_ref[s], qh_ref[win]) + bias_ref[...] + apart
        dp_ref[win] = nt(v_ref[s], dah_ref[win])
    d_sum = jnp.zeros((TOK, HEADS * TOK), F32)
    for win in range(8):
        scores = p_ref[win]
        e = jnp.exp(scores - jnp.max(scores, 0, keepdims=True))
        p = e * (1.0 / jnp.sum(e, 0, keepdims=True))
        pb_ref[win] = p.astype(BF)
        d_p = dp_ref[win]
        d_s = p * (d_p - jnp.sum(d_p * p, 0, keepdims=True))
        d_sum += d_s
        dsb_ref[win] = d_s.astype(BF)
    for win, s in enumerate(windows):
        attn_ref[s] = own_head(tn(pb_ref[win], v_ref[s])).astype(BF)
        dv_ref[s] = nn(pb_ref[win], dah_ref[win]).astype(BF)
        dq_ref[s] = (own_head(tn(dsb_ref[win], k_ref[s])) * scale).astype(BF)
        dk_ref[s] = nn(dsb_ref[win], qh_ref[win]).astype(BF)

    parts = [a for pair in range(3) for a in split(d_sum[:, 128 * pair : 128 * pair + 128])]
    spread = nn(jnp.concatenate(parts, axis=0), spread_pair())
    lines = []
    for pair in range(3):
        both = spread[128 * pair : 128 * pair + TOK] + spread[128 * pair + TOK : 128 * pair + 128]
        lines += [offset_sums(both[:, 0:128]), offset_sums(both[:, 128:256])]
    lines = jnp.concatenate(lines + [jnp.zeros((2, OFF), F32)], axis=0)
    high, low = split(lines)
    by_entry = nt(jnp.concatenate([high, low], axis=0), perm_ref[...])
    by_entry = by_entry[0:8] + by_entry[8:16]

    dq, dk, dv = dq_ref[...], dk_ref[...], dv_ref[...]
    d_normed = nt(dq, w_q) + nt(dk, w_k) + nt(dv, w_v)
    xhat = xhat_ref[...]
    norm_scale = jnp.sum(d_normed * xhat, 0, keepdims=True)
    norm_bias = jnp.sum(d_normed, 0, keepdims=True)
    d_hat = d_normed * ls
    mean_hat = jnp.sum(d_hat, -1, keepdims=True) * (1.0 / CHAN)
    mean_mix = jnp.sum(d_hat * xhat, -1, keepdims=True) * (1.0 / CHAN)
    d_shifted = rstd_ref[...] * (d_hat - mean_hat - xhat * mean_mix)
    for win in range(8):
        wr, wc = win // 4, win % 4
        block = d_shifted[TOK * win : TOK * win + TOK].reshape(WIN, WIN, CHAN)
        ds_ref[WIN * wr : WIN * wr + WIN, WIN * wc : WIN * wc + WIN, :] = block
    edge_ref[...] = ds_ref[ROWS - SHIFT : ROWS].astype(BF)

    normed = normed_ref[...].T
    weights = jnp.concatenate(
        [nn(normed, dq), nn(normed, dk), nn(normed, dv), tn(attn_ref[...], grad_ref[...])], axis=1
    )
    sums = [jnp.sum(a.astype(F32), 0, keepdims=True) for a in (dq, dk, dv)] + [grad_proj_bias]
    small = jnp.concatenate(
        [
            jnp.concatenate(sums, axis=1),
            jnp.concatenate([norm_scale, norm_bias, jnp.zeros((1, 2 * CHAN), F32)], axis=1),
            jnp.concatenate([by_entry[0:1], by_entry[1:2], by_entry[2:3]], axis=1),
            jnp.concatenate([by_entry[3:4], by_entry[4:5], by_entry[5:6]], axis=1),
        ],
        axis=0,
    )
    high = small.astype(BF).astype(F32)
    small = jnp.concatenate([high, small - high], axis=0)
    packed = jnp.concatenate([weights, small], axis=0)
    for chunk in range(30):
        tiles = []
        for tile in range(5 * chunk, 5 * chunk + 5):
            r, c = tile // 6, tile % 6
            tiles.append(packed[8 * r : 8 * r + 8, 128 * c : 128 * c + 128])
        pack_ref[chunk] = jnp.concatenate(tiles, axis=0).astype(BF)
    pack_ref[30:CHUNKS] = jnp.zeros((CHUNKS - 30, PACK, 128), BF)


def add_up(ref, count):
    total = ref[0].astype(F32)
    for i in range(1, count):
        total += ref[i].astype(F32)
    return total


def sum_kernel(got_ref, after_ref, out_ref):
    total = add_up(got_ref, got_ref.shape[0]).astype(BF)
    for i in range(out_ref.shape[0]):
        out_ref[i] = total


def sum_edge_kernel(got_ref, above_ref, ds_ref, out_ref, edge_ref):
    total = add_up(got_ref, got_ref.shape[0]).astype(BF)
    for i in range(out_ref.shape[0]):
        out_ref[i] = total
    edge_ref[0:SHIFT] = above_ref[:, COLS - SHIFT : COLS]
    edge_ref[SHIFT:ROWS] = ds_ref[0 : ROWS - SHIFT, COLS - SHIFT : COLS].astype(BF)


def unpack_kernel(
    got_ref, w_ref, wb_ref, p_ref, pb_ref, ns_ref, nb_ref, table_ref, all_ref
):
    for chunk in range(30):
        tiles = got_ref[chunk].astype(F32)
        for tile in range(5 * chunk, 5 * chunk + 5):
            r, c, part = tile // 6, tile % 6, 8 * (tile % 5)
            all_ref[8 * r : 8 * r + 8, 128 * c : 128 * c + 128] = tiles[part : part + 8]
    w_ref[...] = all_ref[0:CHAN, 0 : 3 * CHAN]
    p_ref[...] = all_ref[0:CHAN, 3 * CHAN : 4 * CHAN]
    small = all_ref[CHAN : CHAN + 4, :] + all_ref[CHAN + 4 : CHAN + 8, :]
    wb_ref[...] = small[0, 0 : 3 * CHAN]
    pb_ref[...] = small[0, 3 * CHAN : 4 * CHAN]
    ns_ref[...] = small[1, 0:CHAN]
    nb_ref[...] = small[1, CHAN : 2 * CHAN]
    for h in range(HEADS):
        place = OFF * (h % 3)
        table_ref[h : h + 1, :] = small[2 + h // 3 : 3 + h // 3, place : place + TABLE]


def kernel_call(kernel, out_shape, scratch=(), flops=10**7, **specs):
    return pl.pallas_call(
        kernel,
        out_shape=out_shape,
        scratch_shapes=scratch,
        **specs,
        cost_estimate=pl.CostEstimate(flops=flops, bytes_accessed=10**6, transcendentals=0),
        compiler_params=pltpu.CompilerParams(vmem_limit_bytes=40 * 2**20),
    )


def shape(dims, kind=F32):
    return jax.ShapeDtypeStruct(dims, kind)


def moved(block, axes, distance):
    sizes = [lax.axis_size(a) for a in axes]
    count = sizes[0] * sizes[1]
    return lax.ppermute(block, axes, [((i - distance) % count, i) for i in range(count)])


def moved_corner(block):
    pairs = [
        (8 * ((r + 1) % 8) + (c + 1) % 8, 8 * r + c) for r in range(8) for c in range(8)
    ]
    return lax.ppermute(block, ROW + COL, pairs)


def prepare(*args):
    return kernel_call(
        prepare_kernel,
        (
            shape((TOK, HEADS * TOK)),
            shape((OFF, OFF), BF),
            shape((8, TOK, 128)),
            shape((3, CHAN, CHAN), BF),
            shape((8, 3 * CHAN)),
        ),
    )(*args)


def halos(x, g):
    return kernel_call(
        halo_kernel,
        (
            shape((2, SHIFT, COLS, CHAN), BF),
            shape((2, SHIFT, SHIFT, CHAN), BF),
        ),
    )(x, g)


def main(*args):
    tokens = 8 * TOK
    return kernel_call(
        main_kernel,
        (
            shape((ROWS, COLS, CHAN)),
            shape((SHIFT, COLS, CHAN), BF),
            shape((CHUNKS, PACK, 128), BF),
        ),
        [
            pltpu.VMEM((ROWS + 8, COLS + 8, CHAN), F32),
            pltpu.VMEM((tokens, CHAN), F32),
            pltpu.VMEM((tokens, 1), F32),
        ]
        + [pltpu.VMEM((tokens, CHAN), BF)] * 10
        + [pltpu.VMEM((8, HEADS * TOK, CHAN), BF)] * 2
        + [pltpu.VMEM((8, TOK, HEADS * TOK), F32)] * 2
        + [pltpu.VMEM((8, TOK, HEADS * TOK), BF)] * 2,
        flops=10**9,
    )(*args)


def chunk_sum(got, copies, after):
    return kernel_call(sum_kernel, shape((copies,) + got.shape[1:], BF))(got, after)


def chunk_sum_edge(got, copies, above, d_shifted):
    return kernel_call(
        sum_edge_kernel,
        (shape((copies,) + got.shape[1:], BF), shape((ROWS, SHIFT, CHAN), BF)),
    )(got, above, d_shifted)


def unpack(got):
    return kernel_call(
        unpack_kernel,
        (
            shape((CHAN, 3 * CHAN)),
            shape((3 * CHAN,)),
            shape((CHAN, CHAN)),
            shape((CHAN,)),
            shape((CHAN,)),
            shape((CHAN,)),
            shape((HEADS, TABLE)),
        ),
        [pltpu.VMEM((CHAN + 8, 4 * CHAN), F32)],
    )(got)


def on_device(
    block_input,
    grad_out,
    region_ids,
    layernorm_scale,
    layernorm_bias,
    qkv_weight,
    qkv_bias,
    proj_weight,
    bias_table,
    position_index,
):
    x, g = block_input[0], grad_out[0]
    col = moved(jnp.stack([x[:, :SHIFT], g[:, :SHIFT]]), COL, -1)
    row, corner = halos(x, g)
    row, corner = moved(row, ROW, -1), moved_corner(corner)
    bias, perm, apart, parts, rows = prepare(
        position_index, bias_table.T, region_ids, qkv_weight, layernorm_scale, layernorm_bias, qkv_bias
    )
    d_shifted, edge, packed = main(
        x, g, row, col, corner, parts, proj_weight, bias, perm, apart, rows
    )
    above = moved(edge, ROW, 1)
    got = lax.all_to_all(packed, FIRST, 0, 0, tiled=True)
    part = chunk_sum(got, 16, above)
    got = lax.all_to_all(part, SECOND, 0, 0, tiled=True)
    whole, edge = chunk_sum_edge(got, CHUNKS, above, d_shifted)
    left = moved(edge, COL, 1)
    gathered = lax.all_to_all(whole, FIRST, 0, 0, tiled=True)
    back = jnp.concatenate([above.astype(F32), d_shifted[: ROWS - SHIFT]], axis=0)
    back = jnp.concatenate([left.astype(F32), back[:, : COLS - SHIFT]], axis=1)
    grad_x = (g.astype(F32) + back).astype(BF)[None]
    w, wb, p, pb, ns, nb, table = unpack(gathered)
    return (grad_x, w, wb, p, pb, ns, nb, table.T)


def solution(mesh):
    fine = Mesh(mesh.devices.reshape(8, 4, 2, 2, 4), ("y", "zl", "c", "zh", "x"))
    tiles = P("y", ROW, COL, None)
    return jax.shard_map(
        on_device,
        mesh=fine,
        in_specs=(tiles, tiles, P(ROW, COL), P(), P(), P(), P(), P(), P(), P()),
        out_specs=(tiles, P(), P(), P(), P(), P(), P(), P()),
        check_vma=False,
    )
```

```python
import jax
import jax.numpy as jnp
from jax import lax
from jax.experimental import pallas as pl
from jax.experimental.pallas import tpu as pltpu
from jax.sharding import Mesh, PartitionSpec as P

WIN = 8
SHIFT = 4
TOK = 64
HEADS = 6
CHAN = 192
DIM = 32
ROWS = 16
COLS = 32
TABLE = 225
OFF = 256
CHUNKS = 32
PACK = 40
BF = jnp.bfloat16
F32 = jnp.float32
HIGH = lax.Precision.HIGHEST

FIRST = ("y", "x")
SECOND = ("zl", "c", "zh")
ROW = ("zl", "c")
COL = ("zh", "x")


def nn(a, b, precision=None):
    return lax.dot_general(a, b, (((1,), (0,)), ((), ())), precision=precision, preferred_element_type=F32)


def nt(a, b, precision=None):
    return lax.dot_general(a, b, (((1,), (1,)), ((), ())), precision=precision, preferred_element_type=F32)


def tn(a, b, precision=None):
    return lax.dot_general(a, b, (((0,), (0,)), ((), ())), precision=precision, preferred_element_type=F32)


def iota(shape, dim):
    return lax.broadcasted_iota(jnp.int32, shape, dim)


def split(a):
    high = a.astype(BF)
    return high, (a - high.astype(F32)).astype(BF)


def spread_pair():
    source, lane = iota((128, 256), 0), iota((128, 256), 1)
    head, a = source // TOK, source % TOK
    return (lane == 128 * head + 127 - (16 * (a // WIN) + a % WIN)).astype(BF)


def squeeze_pair():
    source, lane = iota((256, 128), 0), iota((256, 128), 1)
    head, a = lane // TOK, lane % TOK
    return (source == 128 * head + 16 * (a // WIN) + a % WIN).astype(F32)


def offset_sums(spread):
    blank = jnp.zeros((WIN, 128), F32)
    total = jnp.zeros((WIN, OFF), F32)
    for i in range(WIN):
        wide = jnp.concatenate([spread[WIN * i : WIN * i + WIN], blank], axis=1)
        total += pltpu.roll(wide, 16 * i, 1) if i else wide
    return jnp.sum(pltpu.roll(total, 0, 1, stride=1, stride_axis=0), 0, keepdims=True)


def prepare_kernel(
    pos_ref,
    table_ref,
    ids_ref,
    w_ref,
    ls_ref,
    lb_ref,
    qb_ref,
    bias_ref,
    perm_ref,
    apart_ref,
    parts_ref,
    rows_ref,
):
    rows_ref[0, 0:CHAN] = ls_ref[...]
    rows_ref[1, 0:CHAN] = lb_ref[...]
    rows_ref[2, :] = qb_ref[...]
    w = w_ref[...]
    for i in range(3):
        parts_ref[i] = w[:, CHAN * i : CHAN * i + CHAN]

    token, tile_row = iota((8 * TOK, ROWS), 0), iota((8 * TOK, ROWS), 1)
    window, inside = token // TOK, token % TOK
    pick_row = (tile_row == WIN * (window // 4) + inside // WIN).astype(BF)
    spread_ids = nn(pick_row, ids_ref[...].astype(F32).astype(BF))
    token, tile_col = iota((8 * TOK, COLS), 0), iota((8 * TOK, COLS), 1)
    window, inside = token // TOK, token % TOK
    pick_col = tile_col == WIN * (window % 4) + inside % WIN
    ids = jnp.sum(jnp.where(pick_col, spread_ids, 0.0), -1, keepdims=True)
    region = (ids == iota((8 * TOK, 16), 1).astype(F32)).astype(BF)
    for win in range(8):
        own = region[TOK * win : TOK * win + TOK]
        apart_ref[win] = nt(own, jnp.concatenate([own, own], axis=0)) * 100.0 - 100.0

    pos = pos_ref[...]
    both = jnp.concatenate([pos, jnp.ones_like(pos)], axis=1).astype(F32).astype(BF)
    spread = nn(both, spread_pair())
    count = offset_sums(spread[:, 128:256])
    entry_ahead = offset_sums(spread[:, 0:128])
    back = pos.astype(F32).T
    back = jnp.concatenate([back, back], axis=1).astype(BF)
    entry_back = offset_sums(nn(back, spread_pair())[:, 0:128])

    def entry(total):
        whole = jnp.floor(total / jnp.maximum(count, 1.0) + 0.5).astype(jnp.int32)
        return jnp.where(count > 0.5, whole, -1)

    t = iota((OFF, OFF), 0)
    perm_ref[...] = (t == entry(entry_back)).astype(BF)
    perm_ahead = (iota((TABLE, OFF), 0) == entry(entry_ahead)).astype(F32)
    by_offset = nn(table_ref[...], perm_ahead, HIGH)
    squeeze = squeeze_pair()
    for pair in range(HEADS // 2):
        halves = []
        for h in (2 * pair, 2 * pair + 1):
            line = jnp.broadcast_to(by_offset[h : h + 1], (WIN, OFF))
            line = pltpu.roll(line, 129, 1, stride=1, stride_axis=0)
            shifts = [line] + [pltpu.roll(line, 16 * i, 1) for i in range(1, WIN)]
            halves.append(jnp.concatenate([a[:, 0:128] for a in shifts], axis=0))
        bias_ref[:, 128 * pair : 128 * pair + 128] = nn(
            jnp.concatenate(halves, axis=1), squeeze, HIGH
        )


def halo_kernel(x_ref, g_ref, row_ref, corner_ref):
    for i, ref in enumerate((x_ref, g_ref)):
        tile = ref[0:SHIFT]
        row_ref[i] = tile
        corner_ref[i] = tile[:, 0:SHIFT]


def main_kernel(
    x_ref,
    g_ref,
    row_ref,
    col_ref,
    corner_ref,
    parts_ref,
    wp_ref,
    bias_ref,
    perm_ref,
    apart_ref,
    rows_ref,
    ds_ref,
    pack_ref,
    ext_ref,
    xhat_ref,
    rstd_ref,
    normed_ref,
    grad_ref,
    q_ref,
    k_ref,
    v_ref,
    da_ref,
    attn_ref,
    dq_ref,
    dk_ref,
    dv_ref,
    qh_ref,
    dah_ref,
    p_ref,
    dp_ref,
    pb_ref,
    dsb_ref,
):
    scale = DIM ** (-0.5)

    def windowed(tile_ref, which):
        ext_ref[0:ROWS, 0:COLS, :] = tile_ref[...].astype(F32)
        ext_ref[ROWS : ROWS + SHIFT, 0:COLS, :] = row_ref[which].astype(F32)
        ext_ref[0:ROWS, COLS : COLS + SHIFT, :] = col_ref[which].astype(F32)
        ext_ref[ROWS : ROWS + SHIFT, COLS : COLS + SHIFT, :] = corner_ref[which].astype(F32)
        pieces = []
        for wr in range(ROWS // WIN):
            for wc in range(COLS // WIN):
                r, c = WIN * wr + SHIFT, WIN * wc + SHIFT
                pieces.append(ext_ref[r : r + WIN, c : c + WIN, :].reshape(TOK, CHAN))
        return jnp.concatenate(pieces, axis=0)

    grad = windowed(g_ref, 1)
    grad_ref[...] = grad.astype(BF)
    grad_proj_bias = jnp.sum(grad, 0, keepdims=True)
    x = windowed(x_ref, 0)
    mean = jnp.sum(x, -1, keepdims=True) * (1.0 / CHAN)
    centered = x - mean
    rstd = lax.rsqrt(jnp.sum(centered * centered, -1, keepdims=True) * (1.0 / CHAN) + 1e-05)
    xhat = centered * rstd
    xhat_ref[...] = xhat
    rstd_ref[...] = rstd
    ls, lb, qb = rows_ref[0:1, 0:CHAN], rows_ref[1:2, 0:CHAN], rows_ref[2:3, :]
    normed = (xhat * ls + lb).astype(BF)
    normed_ref[...] = normed
    w_q, w_k, w_v = parts_ref[0], parts_ref[1], parts_ref[2]
    q_ref[...] = ((nn(normed, w_q) + qb[:, 0:CHAN]) * scale).astype(BF)
    k_ref[...] = (nn(normed, w_k) + qb[:, CHAN : 2 * CHAN]).astype(BF)
    v_ref[...] = (nn(normed, w_v) + qb[:, 2 * CHAN : 3 * CHAN]).astype(BF)
    da_ref[...] = nt(grad_ref[...], wp_ref[...]).astype(BF)

    head_of = iota((TOK, CHAN), 1) // DIM

    def by_head(a):
        zero = jnp.zeros_like(a)
        return jnp.concatenate([jnp.where(head_of == h, a, zero) for h in range(HEADS)], axis=0)

    def own_head(a):
        total = jnp.where(head_of == 0, a[0:TOK], 0.0)
        for h in range(1, HEADS):
            total = jnp.where(head_of == h, a[TOK * h : TOK * h + TOK], total)
        return total

    windows = [slice(TOK * win, TOK * win + TOK) for win in range(8)]
    for win, s in enumerate(windows):
        qh_ref[win] = by_head(q_ref[s])
        dah_ref[win] = by_head(da_ref[s])
    for win, s in enumerate(windows):
        apart = jnp.concatenate([apart_ref[win]] * 3, axis=1)
        p_ref[win] = nt(k_ref[s], qh_ref[win]) + bias_ref[...] + apart
        dp_ref[win] = nt(v_ref[s], dah_ref[win])
    d_sum = jnp.zeros((TOK, HEADS * TOK), F32)
    for win in range(8):
        scores = p_ref[win]
        e = jnp.exp(scores - jnp.max(scores, 0, keepdims=True))
        p = e * (1.0 / jnp.sum(e, 0, keepdims=True))
        pb_ref[win] = p.astype(BF)
        d_p = dp_ref[win]
        d_s = p * (d_p - jnp.sum(d_p * p, 0, keepdims=True))
        d_sum += d_s
        dsb_ref[win] = d_s.astype(BF)
    for win, s in enumerate(windows):
        attn_ref[s] = own_head(tn(pb_ref[win], v_ref[s])).astype(BF)
        dv_ref[s] = nn(pb_ref[win], dah_ref[win]).astype(BF)
        dq_ref[s] = (own_head(tn(dsb_ref[win], k_ref[s])) * scale).astype(BF)
        dk_ref[s] = nn(dsb_ref[win], qh_ref[win]).astype(BF)

    parts = [a for pair in range(3) for a in split(d_sum[:, 128 * pair : 128 * pair + 128])]
    spread = nn(jnp.concatenate(parts, axis=0), spread_pair())
    lines = []
    for pair in range(3):
        both = spread[128 * pair : 128 * pair + TOK] + spread[128 * pair + TOK : 128 * pair + 128]
        lines += [offset_sums(both[:, 0:128]), offset_sums(both[:, 128:256])]
    lines = jnp.concatenate(lines + [jnp.zeros((2, OFF), F32)], axis=0)
    high, low = split(lines)
    by_entry = nt(jnp.concatenate([high, low], axis=0), perm_ref[...])
    by_entry = by_entry[0:8] + by_entry[8:16]

    dq, dk, dv = dq_ref[...], dk_ref[...], dv_ref[...]
    d_normed = nt(dq, w_q) + nt(dk, w_k) + nt(dv, w_v)
    xhat = xhat_ref[...]
    norm_scale = jnp.sum(d_normed * xhat, 0, keepdims=True)
    norm_bias = jnp.sum(d_normed, 0, keepdims=True)
    d_hat = d_normed * ls
    mean_hat = jnp.sum(d_hat, -1, keepdims=True) * (1.0 / CHAN)
    mean_mix = jnp.sum(d_hat * xhat, -1, keepdims=True) * (1.0 / CHAN)
    d_shifted = rstd_ref[...] * (d_hat - mean_hat - xhat * mean_mix)
    for win in range(8):
        wr, wc = win // 4, win % 4
        block = d_shifted[TOK * win : TOK * win + TOK].reshape(WIN, WIN, CHAN)
        ds_ref[WIN * wr : WIN * wr + WIN, WIN * wc : WIN * wc + WIN, :] = block

    normed = normed_ref[...].T
    weights = jnp.concatenate(
        [nn(normed, dq), nn(normed, dk), nn(normed, dv), tn(attn_ref[...], grad_ref[...])], axis=1
    )
    sums = [jnp.sum(a.astype(F32), 0, keepdims=True) for a in (dq, dk, dv)] + [grad_proj_bias]
    small = jnp.concatenate(
        [
            jnp.concatenate(sums, axis=1),
            jnp.concatenate([norm_scale, norm_bias, jnp.zeros((1, 2 * CHAN), F32)], axis=1),
            jnp.concatenate([by_entry[0:1], by_entry[1:2], by_entry[2:3]], axis=1),
            jnp.concatenate([by_entry[3:4], by_entry[4:5], by_entry[5:6]], axis=1),
        ],
        axis=0,
    )
    high = small.astype(BF).astype(F32)
    small = jnp.concatenate([high, small - high], axis=0)
    packed = jnp.concatenate([weights, small], axis=0)
    for chunk in range(30):
        tiles = []
        for tile in range(5 * chunk, 5 * chunk + 5):
            r, c = tile // 6, tile % 6
            tiles.append(packed[8 * r : 8 * r + 8, 128 * c : 128 * c + 128])
        pack_ref[chunk] = jnp.concatenate(tiles, axis=0).astype(BF)
    pack_ref[30:CHUNKS] = jnp.zeros((CHUNKS - 30, PACK, 128), BF)


def add_up(ref, count):
    total = ref[0].astype(F32)
    for i in range(1, count):
        total += ref[i].astype(F32)
    return total


def part_sum(got_ref, place_ref):
    total = add_up(got_ref, got_ref.shape[0])
    tiles = []
    for i in range(PACK // 8):
        tile = total[8 * i : 8 * i + 8]
        whole = tile + pltpu.roll(tile, 4, 0)
        high = whole.astype(BF).astype(F32)
        parts = jnp.where(iota((8, 128), 0) < 4, high, whole - high)
        tiles.append(jnp.where(place_ref[0] * (PACK // 8) + i >= 6 * CHAN // 8, parts, tile))
    return jnp.concatenate(tiles, axis=0).astype(BF)


def sum_kernel(got_ref, ds_ref, place_ref, out_ref, edge_ref):
    total = part_sum(got_ref, place_ref)
    for i in range(out_ref.shape[0]):
        out_ref[i] = total
    edge_ref[...] = ds_ref[ROWS - SHIFT : ROWS].astype(BF)


def sum_edge_kernel(got_ref, above_ref, ds_ref, place_ref, out_ref, edge_ref):
    total = part_sum(got_ref, place_ref)
    for i in range(out_ref.shape[0]):
        out_ref[i] = total
    edge_ref[0:SHIFT] = above_ref[:, COLS - SHIFT : COLS]
    edge_ref[SHIFT:ROWS] = ds_ref[0 : ROWS - SHIFT, COLS - SHIFT : COLS].astype(BF)


def unpack_kernel(
    got_ref, w_ref, wb_ref, p_ref, pb_ref, ns_ref, nb_ref, table_ref, all_ref
):
    for chunk in range(30):
        tiles = got_ref[chunk].astype(F32)
        for tile in range(5 * chunk, 5 * chunk + 5):
            r, c, part = tile // 6, tile % 6, 8 * (tile % 5)
            all_ref[8 * r : 8 * r + 8, 128 * c : 128 * c + 128] = tiles[part : part + 8]
    w_ref[...] = all_ref[0:CHAN, 0 : 3 * CHAN]
    p_ref[...] = all_ref[0:CHAN, 3 * CHAN : 4 * CHAN]
    small = all_ref[CHAN : CHAN + 4, :] + all_ref[CHAN + 4 : CHAN + 8, :]
    wb_ref[...] = small[0, 0 : 3 * CHAN]
    pb_ref[...] = small[0, 3 * CHAN : 4 * CHAN]
    ns_ref[...] = small[1, 0:CHAN]
    nb_ref[...] = small[1, CHAN : 2 * CHAN]
    for h in range(HEADS):
        place = OFF * (h % 3)
        table_ref[h : h + 1, :] = small[2 + h // 3 : 3 + h // 3, place : place + TABLE]


def kernel_call(kernel, out_shape, scratch=(), flops=10**7, **specs):
    return pl.pallas_call(
        kernel,
        out_shape=out_shape,
        scratch_shapes=scratch,
        **specs,
        cost_estimate=pl.CostEstimate(flops=flops, bytes_accessed=10**6, transcendentals=0),
        compiler_params=pltpu.CompilerParams(vmem_limit_bytes=40 * 2**20),
    )


def shape(dims, kind=F32):
    return jax.ShapeDtypeStruct(dims, kind)


def moved(block, axes, distance):
    sizes = [lax.axis_size(a) for a in axes]
    count = sizes[0] * sizes[1]
    return lax.ppermute(block, axes, [((i - distance) % count, i) for i in range(count)])


def moved_corner(block):
    pairs = [
        (8 * ((r + 1) % 8) + (c + 1) % 8, 8 * r + c) for r in range(8) for c in range(8)
    ]
    return lax.ppermute(block, ROW + COL, pairs)


def prepare(*args):
    return kernel_call(
        prepare_kernel,
        (
            shape((TOK, HEADS * TOK)),
            shape((OFF, OFF), BF),
            shape((8, TOK, 128)),
            shape((3, CHAN, CHAN), BF),
            shape((8, 3 * CHAN)),
        ),
    )(*args)


def halos(x, g):
    return kernel_call(
        halo_kernel,
        (
            shape((2, SHIFT, COLS, CHAN), BF),
            shape((2, SHIFT, SHIFT, CHAN), BF),
        ),
    )(x, g)


def main(*args):
    tokens = 8 * TOK
    return kernel_call(
        main_kernel,
        (
            shape((ROWS, COLS, CHAN)),
            shape((CHUNKS, PACK, 128), BF),
        ),
        [
            pltpu.VMEM((ROWS + 8, COLS + 8, CHAN), F32),
            pltpu.VMEM((tokens, CHAN), F32),
            pltpu.VMEM((tokens, 1), F32),
        ]
        + [pltpu.VMEM((tokens, CHAN), BF)] * 10
        + [pltpu.VMEM((8, HEADS * TOK, CHAN), BF)] * 2
        + [pltpu.VMEM((8, TOK, HEADS * TOK), F32)] * 2
        + [pltpu.VMEM((8, TOK, HEADS * TOK), BF)] * 2,
        flops=10**9,
    )(*args)


SMALL = pl.BlockSpec(memory_space=pltpu.SMEM)
WHOLE = pl.BlockSpec(memory_space=pltpu.VMEM)


def chunk_sum(got, copies, d_shifted, place):
    return kernel_call(
        sum_kernel,
        (shape((copies,) + got.shape[1:], BF), shape((SHIFT, COLS, CHAN), BF)),
        in_specs=[WHOLE, WHOLE, SMALL],
    )(got, d_shifted, place)


def chunk_sum_edge(got, copies, above, d_shifted, place):
    return kernel_call(
        sum_edge_kernel,
        (shape((copies,) + got.shape[1:], BF), shape((ROWS, SHIFT, CHAN), BF)),
        in_specs=[WHOLE, WHOLE, WHOLE, SMALL],
    )(got, above, d_shifted, place)


def unpack(got):
    return kernel_call(
        unpack_kernel,
        (
            shape((CHAN, 3 * CHAN)),
            shape((3 * CHAN,)),
            shape((CHAN, CHAN)),
            shape((CHAN,)),
            shape((CHAN,)),
            shape((CHAN,)),
            shape((HEADS, TABLE)),
        ),
        [pltpu.VMEM((CHAN + 8, 4 * CHAN), F32)],
    )(got)


def on_device(
    block_input,
    grad_out,
    region_ids,
    layernorm_scale,
    layernorm_bias,
    qkv_weight,
    qkv_bias,
    proj_weight,
    bias_table,
    position_index,
):
    x, g = block_input[0], grad_out[0]
    col = moved(jnp.stack([x[:, :SHIFT], g[:, :SHIFT]]), COL, -1)
    row, corner = halos(x, g)
    row, corner = moved(row, ROW, -1), moved_corner(corner)
    bias, perm, apart, parts, rows = prepare(
        position_index, bias_table.T, region_ids, qkv_weight, layernorm_scale, layernorm_bias, qkv_bias
    )
    place = lax.axis_index(FIRST).astype(jnp.int32)[None]
    rows, place = lax.optimization_barrier((rows, place))
    d_shifted, packed = main(
        x, g, row, col, corner, parts, proj_weight, bias, perm, apart, rows
    )
    got = lax.all_to_all(packed, FIRST, 0, 0, tiled=True)
    part, edge = chunk_sum(got, 16, d_shifted, place)
    above = moved(edge, ROW, 1)
    got = lax.all_to_all(part, SECOND, 0, 0, tiled=True)
    whole, edge = chunk_sum_edge(got, CHUNKS, above, d_shifted, place)
    left = moved(edge, COL, 1)
    gathered = lax.all_to_all(whole, FIRST, 0, 0, tiled=True)
    back = jnp.concatenate([above.astype(F32), d_shifted[: ROWS - SHIFT]], axis=0)
    back = jnp.concatenate([left.astype(F32), back[:, : COLS - SHIFT]], axis=1)
    grad_x = (g.astype(F32) + back).astype(BF)[None]
    w, wb, p, pb, ns, nb, table = unpack(gathered)
    return (grad_x, w, wb, p, pb, ns, nb, table.T)


def solution(mesh):
    fine = Mesh(mesh.devices.reshape(8, 4, 2, 2, 4), ("y", "zl", "c", "zh", "x"))
    tiles = P("y", ROW, COL, None)
    return jax.shard_map(
        on_device,
        mesh=fine,
        in_specs=(tiles, tiles, P(ROW, COL), P(), P(), P(), P(), P(), P(), P()),
        out_specs=(tiles, P(), P(), P(), P(), P(), P(), P()),
        check_vma=False,
    )
```

```python
import jax
import jax.numpy as jnp
from jax import lax
from jax.experimental import pallas as pl
from jax.experimental.pallas import tpu as pltpu
from jax.sharding import Mesh, PartitionSpec as P

WIN = 8
SHIFT = 4
TOK = 64
HEADS = 6
CHAN = 192
DIM = 32
ROWS = 16
COLS = 32
TABLE = 225
OFF = 256
CHUNKS = 32
PACK = 40
BF = jnp.bfloat16
F32 = jnp.float32
HIGH = lax.Precision.HIGHEST

FIRST = ("y", "x")
SECOND = ("zl", "c", "zh")
ROW = ("zl", "c")
COL = ("zh", "x")


def nn(a, b, precision=None):
    return lax.dot_general(a, b, (((1,), (0,)), ((), ())), precision=precision, preferred_element_type=F32)


def nt(a, b, precision=None):
    return lax.dot_general(a, b, (((1,), (1,)), ((), ())), precision=precision, preferred_element_type=F32)


def tn(a, b, precision=None):
    return lax.dot_general(a, b, (((0,), (0,)), ((), ())), precision=precision, preferred_element_type=F32)


def iota(shape, dim):
    return lax.broadcasted_iota(jnp.int32, shape, dim)


def split(a):
    high = a.astype(BF)
    return high, (a - high.astype(F32)).astype(BF)


def spread_pair():
    source, lane = iota((128, 256), 0), iota((128, 256), 1)
    head, a = source // TOK, source % TOK
    return (lane == 128 * head + 127 - (16 * (a // WIN) + a % WIN)).astype(BF)


def squeeze_pair():
    source, lane = iota((256, 128), 0), iota((256, 128), 1)
    head, a = lane // TOK, lane % TOK
    return (source == 128 * head + 16 * (a // WIN) + a % WIN).astype(F32)


def offset_sums(spread):
    blank = jnp.zeros((WIN, 128), F32)
    total = jnp.zeros((WIN, OFF), F32)
    for i in range(WIN):
        wide = jnp.concatenate([spread[WIN * i : WIN * i + WIN], blank], axis=1)
        total += pltpu.roll(wide, 16 * i, 1) if i else wide
    return jnp.sum(pltpu.roll(total, 0, 1, stride=1, stride_axis=0), 0, keepdims=True)


def prepare_kernel(
    pos_ref,
    table_ref,
    ids_ref,
    w_ref,
    ls_ref,
    lb_ref,
    qb_ref,
    bias_ref,
    perm_ref,
    apart_ref,
    parts_ref,
    rows_ref,
):
    rows_ref[0, 0:CHAN] = ls_ref[...]
    rows_ref[1, 0:CHAN] = lb_ref[...]
    rows_ref[2, :] = qb_ref[...]
    w = w_ref[...]
    for i in range(3):
        parts_ref[i] = w[:, CHAN * i : CHAN * i + CHAN]

    token, tile_row = iota((8 * TOK, ROWS), 0), iota((8 * TOK, ROWS), 1)
    window, inside = token // TOK, token % TOK
    pick_row = (tile_row == WIN * (window // 4) + inside // WIN).astype(BF)
    spread_ids = nn(pick_row, ids_ref[...].astype(F32).astype(BF))
    token, tile_col = iota((8 * TOK, COLS), 0), iota((8 * TOK, COLS), 1)
    window, inside = token // TOK, token % TOK
    pick_col = tile_col == WIN * (window % 4) + inside % WIN
    ids = jnp.sum(jnp.where(pick_col, spread_ids, 0.0), -1, keepdims=True)
    region = (ids == iota((8 * TOK, 16), 1).astype(F32)).astype(BF)
    for win in range(8):
        own = region[TOK * win : TOK * win + TOK]
        apart_ref[win] = nt(own, jnp.concatenate([own, own], axis=0)) * 100.0 - 100.0

    pos = pos_ref[...]
    both = jnp.concatenate([pos, jnp.ones_like(pos)], axis=1).astype(F32).astype(BF)
    spread = nn(both, spread_pair())
    count = offset_sums(spread[:, 128:256])
    entry_ahead = offset_sums(spread[:, 0:128])
    back = pos.astype(F32).T
    back = jnp.concatenate([back, back], axis=1).astype(BF)
    entry_back = offset_sums(nn(back, spread_pair())[:, 0:128])

    def entry(total):
        whole = jnp.floor(total / jnp.maximum(count, 1.0) + 0.5).astype(jnp.int32)
        return jnp.where(count > 0.5, whole, -1)

    t = iota((OFF, OFF), 0)
    perm_ref[...] = (t == entry(entry_back)).astype(BF)
    perm_ahead = (iota((TABLE, OFF), 0) == entry(entry_ahead)).astype(F32)
    by_offset = nn(table_ref[...], perm_ahead, HIGH)
    squeeze = squeeze_pair()
    for pair in range(HEADS // 2):
        halves = []
        for h in (2 * pair, 2 * pair + 1):
            line = jnp.broadcast_to(by_offset[h : h + 1], (WIN, OFF))
            line = pltpu.roll(line, 129, 1, stride=1, stride_axis=0)
            shifts = [line] + [pltpu.roll(line, 16 * i, 1) for i in range(1, WIN)]
            halves.append(jnp.concatenate([a[:, 0:128] for a in shifts], axis=0))
        bias_ref[:, 128 * pair : 128 * pair + 128] = nn(
            jnp.concatenate(halves, axis=1), squeeze, HIGH
        )


def halo_kernel(x_ref, g_ref, row_ref, corner_ref):
    for i, ref in enumerate((x_ref, g_ref)):
        tile = ref[0:SHIFT]
        row_ref[i] = tile
        corner_ref[i] = tile[:, 0:SHIFT]


def main_kernel(
    x_ref,
    g_ref,
    row_ref,
    col_ref,
    corner_ref,
    parts_ref,
    wp_ref,
    bias_ref,
    perm_ref,
    apart_ref,
    rows_ref,
    dn_ref,
    xhat_ref,
    rstd_ref,
    pack_ref,
    ext_ref,
    normed_ref,
    grad_ref,
    q_ref,
    k_ref,
    v_ref,
    da_ref,
    attn_ref,
    dq_ref,
    dk_ref,
    dv_ref,
    qh_ref,
    dah_ref,
    p_ref,
    dp_ref,
    pb_ref,
    dsb_ref,
):
    scale = DIM ** (-0.5)

    def windowed(tile_ref, which):
        ext_ref[0:ROWS, 0:COLS, :] = tile_ref[...].astype(F32)
        ext_ref[ROWS : ROWS + SHIFT, 0:COLS, :] = row_ref[which].astype(F32)
        ext_ref[0:ROWS, COLS : COLS + SHIFT, :] = col_ref[which].astype(F32)
        ext_ref[ROWS : ROWS + SHIFT, COLS : COLS + SHIFT, :] = corner_ref[which].astype(F32)
        pieces = []
        for wr in range(ROWS // WIN):
            for wc in range(COLS // WIN):
                r, c = WIN * wr + SHIFT, WIN * wc + SHIFT
                pieces.append(ext_ref[r : r + WIN, c : c + WIN, :].reshape(TOK, CHAN))
        return jnp.concatenate(pieces, axis=0)

    grad = windowed(g_ref, 1)
    grad_ref[...] = grad.astype(BF)
    grad_proj_bias = jnp.sum(grad, 0, keepdims=True)
    x = windowed(x_ref, 0)
    mean = jnp.sum(x, -1, keepdims=True) * (1.0 / CHAN)
    centered = x - mean
    rstd = lax.rsqrt(jnp.sum(centered * centered, -1, keepdims=True) * (1.0 / CHAN) + 1e-05)
    xhat = centered * rstd
    xhat_ref[...] = xhat
    rstd_ref[...] = rstd
    ls, lb, qb = rows_ref[0:1, 0:CHAN], rows_ref[1:2, 0:CHAN], rows_ref[2:3, :]
    normed = (xhat * ls + lb).astype(BF)
    normed_ref[...] = normed
    w_q, w_k, w_v = parts_ref[0], parts_ref[1], parts_ref[2]
    q_ref[...] = ((nn(normed, w_q) + qb[:, 0:CHAN]) * scale).astype(BF)
    k_ref[...] = (nn(normed, w_k) + qb[:, CHAN : 2 * CHAN]).astype(BF)
    v_ref[...] = (nn(normed, w_v) + qb[:, 2 * CHAN : 3 * CHAN]).astype(BF)
    da_ref[...] = nt(grad_ref[...], wp_ref[...]).astype(BF)

    head_of = iota((TOK, CHAN), 1) // DIM

    def by_head(a):
        zero = jnp.zeros_like(a)
        return jnp.concatenate([jnp.where(head_of == h, a, zero) for h in range(HEADS)], axis=0)

    def own_head(a):
        total = jnp.where(head_of == 0, a[0:TOK], 0.0)
        for h in range(1, HEADS):
            total = jnp.where(head_of == h, a[TOK * h : TOK * h + TOK], total)
        return total

    windows = [slice(TOK * win, TOK * win + TOK) for win in range(8)]
    for win, s in enumerate(windows):
        qh_ref[win] = by_head(q_ref[s])
        dah_ref[win] = by_head(da_ref[s])
    for win, s in enumerate(windows):
        apart = jnp.concatenate([apart_ref[win]] * 3, axis=1)
        p_ref[win] = nt(k_ref[s], qh_ref[win]) + bias_ref[...] + apart
        dp_ref[win] = nt(v_ref[s], dah_ref[win])
    d_sum = jnp.zeros((TOK, HEADS * TOK), F32)
    for win in range(8):
        scores = p_ref[win]
        e = jnp.exp(scores - jnp.max(scores, 0, keepdims=True))
        p = e * (1.0 / jnp.sum(e, 0, keepdims=True))
        pb_ref[win] = p.astype(BF)
        d_p = dp_ref[win]
        d_s = p * (d_p - jnp.sum(d_p * p, 0, keepdims=True))
        d_sum += d_s
        dsb_ref[win] = d_s.astype(BF)
    for win, s in enumerate(windows):
        attn_ref[s] = own_head(tn(pb_ref[win], v_ref[s])).astype(BF)
        dv_ref[s] = nn(pb_ref[win], dah_ref[win]).astype(BF)
        dq_ref[s] = (own_head(tn(dsb_ref[win], k_ref[s])) * scale).astype(BF)
        dk_ref[s] = nn(dsb_ref[win], qh_ref[win]).astype(BF)

    parts = [a for pair in range(3) for a in split(d_sum[:, 128 * pair : 128 * pair + 128])]
    spread = nn(jnp.concatenate(parts, axis=0), spread_pair())
    lines = []
    for pair in range(3):
        both = spread[128 * pair : 128 * pair + TOK] + spread[128 * pair + TOK : 128 * pair + 128]
        lines += [offset_sums(both[:, 0:128]), offset_sums(both[:, 128:256])]
    lines = jnp.concatenate(lines + [jnp.zeros((2, OFF), F32)], axis=0)
    high, low = split(lines)
    by_entry = nt(jnp.concatenate([high, low], axis=0), perm_ref[...])
    by_entry = by_entry[0:8] + by_entry[8:16]

    dq, dk, dv = dq_ref[...], dk_ref[...], dv_ref[...]
    d_normed = nt(dq, w_q) + nt(dk, w_k) + nt(dv, w_v)
    xhat = xhat_ref[...]
    norm_scale = jnp.sum(d_normed * xhat, 0, keepdims=True)
    norm_bias = jnp.sum(d_normed, 0, keepdims=True)
    dn_ref[...] = d_normed

    normed = normed_ref[...].T
    weights = jnp.concatenate(
        [nn(normed, dq), nn(normed, dk), nn(normed, dv), tn(attn_ref[...], grad_ref[...])], axis=1
    )
    sums = [jnp.sum(a.astype(F32), 0, keepdims=True) for a in (dq, dk, dv)] + [grad_proj_bias]
    small = jnp.concatenate(
        [
            jnp.concatenate(sums, axis=1),
            jnp.concatenate([norm_scale, norm_bias, jnp.zeros((1, 2 * CHAN), F32)], axis=1),
            jnp.concatenate([by_entry[0:1], by_entry[1:2], by_entry[2:3]], axis=1),
            jnp.concatenate([by_entry[3:4], by_entry[4:5], by_entry[5:6]], axis=1),
        ],
        axis=0,
    )
    high = small.astype(BF).astype(F32)
    small = jnp.concatenate([high, small - high], axis=0)
    packed = jnp.concatenate([weights, small], axis=0)
    for chunk in range(30):
        tiles = []
        for tile in range(5 * chunk, 5 * chunk + 5):
            r, c = tile // 6, tile % 6
            tiles.append(packed[8 * r : 8 * r + 8, 128 * c : 128 * c + 128])
        pack_ref[chunk] = jnp.concatenate(tiles, axis=0).astype(BF)
    pack_ref[30:CHUNKS] = jnp.zeros((CHUNKS - 30, PACK, 128), BF)


def add_up(ref, count):
    total = ref[0].astype(F32)
    for i in range(1, count):
        total += ref[i].astype(F32)
    return total


def part_sum(got_ref, place_ref):
    total = add_up(got_ref, got_ref.shape[0])
    tiles = []
    for i in range(PACK // 8):
        tile = total[8 * i : 8 * i + 8]
        whole = tile + pltpu.roll(tile, 4, 0)
        high = whole.astype(BF).astype(F32)
        parts = jnp.where(iota((8, 128), 0) < 4, high, whole - high)
        tiles.append(jnp.where(place_ref[0] * (PACK // 8) + i >= 6 * CHAN // 8, parts, tile))
    return jnp.concatenate(tiles, axis=0).astype(BF)


def finish_kernel(dn_ref, xhat_ref, rstd_ref, rows_ref, mark_ref, ds_ref, edge_ref):
    xhat = xhat_ref[...]
    d_hat = dn_ref[...] * rows_ref[0:1, 0:CHAN]
    mean_hat = jnp.sum(d_hat, -1, keepdims=True) * (1.0 / CHAN)
    mean_mix = jnp.sum(d_hat * xhat, -1, keepdims=True) * (1.0 / CHAN)
    d_shifted = rstd_ref[...] * (d_hat - mean_hat - xhat * mean_mix)
    for win in range(8):
        wr, wc = win // 4, win % 4
        block = d_shifted[TOK * win : TOK * win + TOK].reshape(WIN, WIN, CHAN)
        ds_ref[WIN * wr : WIN * wr + WIN, WIN * wc : WIN * wc + WIN, :] = block
    edge_ref[...] = ds_ref[ROWS - SHIFT : ROWS].astype(BF)


def sum_kernel(got_ref, place_ref, out_ref, mark_ref):
    mark_ref[...] = jnp.zeros_like(mark_ref)
    total = part_sum(got_ref, place_ref)
    for i in range(out_ref.shape[0]):
        out_ref[i] = total


def sum_edge_kernel(got_ref, above_ref, ds_ref, place_ref, out_ref, edge_ref):
    total = part_sum(got_ref, place_ref)
    for i in range(out_ref.shape[0]):
        out_ref[i] = total
    edge_ref[0:SHIFT] = above_ref[:, COLS - SHIFT : COLS]
    edge_ref[SHIFT:ROWS] = ds_ref[0 : ROWS - SHIFT, COLS - SHIFT : COLS].astype(BF)


def unpack_kernel(
    got_ref, w_ref, wb_ref, p_ref, pb_ref, ns_ref, nb_ref, table_ref, all_ref
):
    for chunk in range(30):
        tiles = got_ref[chunk].astype(F32)
        for tile in range(5 * chunk, 5 * chunk + 5):
            r, c, part = tile // 6, tile % 6, 8 * (tile % 5)
            all_ref[8 * r : 8 * r + 8, 128 * c : 128 * c + 128] = tiles[part : part + 8]
    w_ref[...] = all_ref[0:CHAN, 0 : 3 * CHAN]
    p_ref[...] = all_ref[0:CHAN, 3 * CHAN : 4 * CHAN]
    small = all_ref[CHAN : CHAN + 4, :] + all_ref[CHAN + 4 : CHAN + 8, :]
    wb_ref[...] = small[0, 0 : 3 * CHAN]
    pb_ref[...] = small[0, 3 * CHAN : 4 * CHAN]
    ns_ref[...] = small[1, 0:CHAN]
    nb_ref[...] = small[1, CHAN : 2 * CHAN]
    for h in range(HEADS):
        place = OFF * (h % 3)
        table_ref[h : h + 1, :] = small[2 + h // 3 : 3 + h // 3, place : place + TABLE]


def kernel_call(kernel, out_shape, scratch=(), flops=10**7, **specs):
    return pl.pallas_call(
        kernel,
        out_shape=out_shape,
        scratch_shapes=scratch,
        **specs,
        cost_estimate=pl.CostEstimate(flops=flops, bytes_accessed=10**6, transcendentals=0),
        compiler_params=pltpu.CompilerParams(vmem_limit_bytes=40 * 2**20),
    )


def shape(dims, kind=F32):
    return jax.ShapeDtypeStruct(dims, kind)


def moved(block, axes, distance):
    sizes = [lax.axis_size(a) for a in axes]
    count = sizes[0] * sizes[1]
    return lax.ppermute(block, axes, [((i - distance) % count, i) for i in range(count)])


def moved_corner(block):
    pairs = [
        (8 * ((r + 1) % 8) + (c + 1) % 8, 8 * r + c) for r in range(8) for c in range(8)
    ]
    return lax.ppermute(block, ROW + COL, pairs)


def prepare(*args):
    return kernel_call(
        prepare_kernel,
        (
            shape((TOK, HEADS * TOK)),
            shape((OFF, OFF), BF),
            shape((8, TOK, 128)),
            shape((3, CHAN, CHAN), BF),
            shape((8, 3 * CHAN)),
        ),
    )(*args)


def halos(x, g):
    return kernel_call(
        halo_kernel,
        (
            shape((2, SHIFT, COLS, CHAN), BF),
            shape((2, SHIFT, SHIFT, CHAN), BF),
        ),
    )(x, g)


def main(*args):
    tokens = 8 * TOK
    return kernel_call(
        main_kernel,
        (
            shape((tokens, CHAN)),
            shape((tokens, CHAN)),
            shape((tokens, 1)),
            shape((CHUNKS, PACK, 128), BF),
        ),
        [
            pltpu.VMEM((ROWS + 8, COLS + 8, CHAN), F32),
        ]
        + [pltpu.VMEM((tokens, CHAN), BF)] * 10
        + [pltpu.VMEM((8, HEADS * TOK, CHAN), BF)] * 2
        + [pltpu.VMEM((8, TOK, HEADS * TOK), F32)] * 2
        + [pltpu.VMEM((8, TOK, HEADS * TOK), BF)] * 2,
        flops=10**9,
    )(*args)


SMALL = pl.BlockSpec(memory_space=pltpu.SMEM)
WHOLE = pl.BlockSpec(memory_space=pltpu.VMEM)


def chunk_sum(got, copies, place):
    return kernel_call(
        sum_kernel,
        (shape((copies,) + got.shape[1:], BF), shape((8, 128))),
        in_specs=[WHOLE, SMALL],
    )(got, place)


def finish(*args):
    return kernel_call(
        finish_kernel, (shape((ROWS, COLS, CHAN)), shape((SHIFT, COLS, CHAN), BF))
    )(*args)


def chunk_sum_edge(got, copies, above, d_shifted, place):
    return kernel_call(
        sum_edge_kernel,
        (shape((copies,) + got.shape[1:], BF), shape((ROWS, SHIFT, CHAN), BF)),
        in_specs=[WHOLE, WHOLE, WHOLE, SMALL],
    )(got, above, d_shifted, place)


def unpack(got):
    return kernel_call(
        unpack_kernel,
        (
            shape((CHAN, 3 * CHAN)),
            shape((3 * CHAN,)),
            shape((CHAN, CHAN)),
            shape((CHAN,)),
            shape((CHAN,)),
            shape((CHAN,)),
            shape((HEADS, TABLE)),
        ),
        [pltpu.VMEM((CHAN + 8, 4 * CHAN), F32)],
    )(got)


def on_device(
    block_input,
    grad_out,
    region_ids,
    layernorm_scale,
    layernorm_bias,
    qkv_weight,
    qkv_bias,
    proj_weight,
    bias_table,
    position_index,
):
    x, g = block_input[0], grad_out[0]
    col = moved(jnp.stack([x[:, :SHIFT], g[:, :SHIFT]]), COL, -1)
    row, corner = halos(x, g)
    row, corner = moved(row, ROW, -1), moved_corner(corner)
    bias, perm, apart, parts, rows = prepare(
        position_index, bias_table.T, region_ids, qkv_weight, layernorm_scale, layernorm_bias, qkv_bias
    )
    place = lax.axis_index(FIRST).astype(jnp.int32)[None]
    rows, place = lax.optimization_barrier((rows, place))
    d_normed, xhat, rstd, packed = main(
        x, g, row, col, corner, parts, proj_weight, bias, perm, apart, rows
    )
    got = lax.all_to_all(packed, FIRST, 0, 0, tiled=True)
    part, mark = chunk_sum(got, 16, place)
    d_shifted, edge = finish(d_normed, xhat, rstd, rows, mark)
    above = moved(edge, ROW, 1)
    got = lax.all_to_all(part, SECOND, 0, 0, tiled=True)
    whole, edge = chunk_sum_edge(got, CHUNKS, above, d_shifted, place)
    left = moved(edge, COL, 1)
    gathered = lax.all_to_all(whole, FIRST, 0, 0, tiled=True)
    back = jnp.concatenate([above.astype(F32), d_shifted[: ROWS - SHIFT]], axis=0)
    back = jnp.concatenate([left.astype(F32), back[:, : COLS - SHIFT]], axis=1)
    grad_x = (g.astype(F32) + back).astype(BF)[None]
    w, wb, p, pb, ns, nb, table = unpack(gathered)
    return (grad_x, w, wb, p, pb, ns, nb, table.T)


def solution(mesh):
    fine = Mesh(mesh.devices.reshape(8, 4, 2, 2, 4), ("y", "zl", "c", "zh", "x"))
    tiles = P("y", ROW, COL, None)
    return jax.shard_map(
        on_device,
        mesh=fine,
        in_specs=(tiles, tiles, P(ROW, COL), P(), P(), P(), P(), P(), P(), P()),
        out_specs=(tiles, P(), P(), P(), P(), P(), P(), P()),
        check_vma=False,
    )
```

```python
import jax
import jax.numpy as jnp
from jax import lax
from jax.experimental import pallas as pl
from jax.experimental.pallas import tpu as pltpu
from jax.sharding import Mesh, PartitionSpec as P

WIN = 8
SHIFT = 4
TOK = 64
HEADS = 6
CHAN = 192
DIM = 32
ROWS = 16
COLS = 32
TABLE = 225
OFF = 256
CHUNKS = 32
PACK = 40
BF = jnp.bfloat16
F32 = jnp.float32
HIGH = lax.Precision.HIGHEST

FIRST = ("y", "x")
SECOND = ("zl", "c", "zh")
ROW = ("zl", "c")
COL = ("zh", "x")


def nn(a, b, precision=None):
    return lax.dot_general(a, b, (((1,), (0,)), ((), ())), precision=precision, preferred_element_type=F32)


def nt(a, b, precision=None):
    return lax.dot_general(a, b, (((1,), (1,)), ((), ())), precision=precision, preferred_element_type=F32)


def tn(a, b, precision=None):
    return lax.dot_general(a, b, (((0,), (0,)), ((), ())), precision=precision, preferred_element_type=F32)


def iota(shape, dim):
    return lax.broadcasted_iota(jnp.int32, shape, dim)


def split(a):
    high = a.astype(BF)
    return high, (a - high.astype(F32)).astype(BF)


def spread_pair():
    source, lane = iota((128, 256), 0), iota((128, 256), 1)
    head, a = source // TOK, source % TOK
    return (lane == 128 * head + 127 - (16 * (a // WIN) + a % WIN)).astype(BF)


def squeeze_pair():
    source, lane = iota((256, 128), 0), iota((256, 128), 1)
    head, a = lane // TOK, lane % TOK
    return (source == 128 * head + 16 * (a // WIN) + a % WIN).astype(F32)


def offset_sums(spread):
    blank = jnp.zeros((WIN, 128), F32)
    total = jnp.zeros((WIN, OFF), F32)
    for i in range(WIN):
        wide = jnp.concatenate([spread[WIN * i : WIN * i + WIN], blank], axis=1)
        total += pltpu.roll(wide, 16 * i, 1) if i else wide
    return jnp.sum(pltpu.roll(total, 0, 1, stride=1, stride_axis=0), 0, keepdims=True)


def prepare_kernel(
    pos_ref,
    table_ref,
    ids_ref,
    w_ref,
    ls_ref,
    lb_ref,
    qb_ref,
    bias_ref,
    perm_ref,
    apart_ref,
    parts_ref,
    rows_ref,
):
    rows_ref[0, 0:CHAN] = ls_ref[...]
    rows_ref[1, 0:CHAN] = lb_ref[...]
    rows_ref[2, :] = qb_ref[...]
    w = w_ref[...]
    for i in range(3):
        parts_ref[i] = w[:, CHAN * i : CHAN * i + CHAN]

    token, tile_row = iota((8 * TOK, ROWS), 0), iota((8 * TOK, ROWS), 1)
    window, inside = token // TOK, token % TOK
    pick_row = (tile_row == WIN * (window // 4) + inside // WIN).astype(BF)
    spread_ids = nn(pick_row, ids_ref[...].astype(F32).astype(BF))
    token, tile_col = iota((8 * TOK, COLS), 0), iota((8 * TOK, COLS), 1)
    window, inside = token // TOK, token % TOK
    pick_col = tile_col == WIN * (window % 4) + inside % WIN
    ids = jnp.sum(jnp.where(pick_col, spread_ids, 0.0), -1, keepdims=True)
    region = (ids == iota((8 * TOK, 16), 1).astype(F32)).astype(BF)
    for win in range(8):
        own = region[TOK * win : TOK * win + TOK]
        apart_ref[win] = nt(own, jnp.concatenate([own, own], axis=0)) * 100.0 - 100.0

    pos = pos_ref[...]
    both = jnp.concatenate([pos, jnp.ones_like(pos)], axis=1).astype(F32).astype(BF)
    spread = nn(both, spread_pair())
    count = offset_sums(spread[:, 128:256])
    entry_ahead = offset_sums(spread[:, 0:128])
    back = pos.astype(F32).T
    back = jnp.concatenate([back, back], axis=1).astype(BF)
    entry_back = offset_sums(nn(back, spread_pair())[:, 0:128])

    def entry(total):
        whole = jnp.floor(total / jnp.maximum(count, 1.0) + 0.5).astype(jnp.int32)
        return jnp.where(count > 0.5, whole, -1)

    t = iota((OFF, OFF), 0)
    perm_ref[...] = (t == entry(entry_back)).astype(BF)
    perm_ahead = (iota((TABLE, OFF), 0) == entry(entry_ahead)).astype(F32)
    by_offset = nn(table_ref[...], perm_ahead, HIGH)
    squeeze = squeeze_pair()
    for pair in range(HEADS // 2):
        halves = []
        for h in (2 * pair, 2 * pair + 1):
            line = jnp.broadcast_to(by_offset[h : h + 1], (WIN, OFF))
            line = pltpu.roll(line, 129, 1, stride=1, stride_axis=0)
            shifts = [line] + [pltpu.roll(line, 16 * i, 1) for i in range(1, WIN)]
            halves.append(jnp.concatenate([a[:, 0:128] for a in shifts], axis=0))
        bias_ref[:, 128 * pair : 128 * pair + 128] = nn(
            jnp.concatenate(halves, axis=1), squeeze, HIGH
        )


def halo_kernel(x_ref, g_ref, row_ref, corner_ref):
    for i, ref in enumerate((x_ref, g_ref)):
        tile = ref[0:SHIFT]
        row_ref[i] = tile
        corner_ref[i] = tile[:, 0:SHIFT]


def main_kernel(
    x_ref,
    g_ref,
    row_ref,
    col_ref,
    corner_ref,
    parts_ref,
    wp_ref,
    bias_ref,
    perm_ref,
    apart_ref,
    rows_ref,
    dn_ref,
    xhat_ref,
    rstd_ref,
    pack_ref,
    ext_ref,
    normed_ref,
    grad_ref,
    q_ref,
    k_ref,
    v_ref,
    da_ref,
    attn_ref,
    dq_ref,
    dk_ref,
    dv_ref,
    qh_ref,
    dah_ref,
    p_ref,
    dp_ref,
    pb_ref,
    dsb_ref,
):
    scale = DIM ** (-0.5)

    def windowed(tile_ref, which):
        ext_ref[0:ROWS, 0:COLS, :] = tile_ref[...].astype(F32)
        ext_ref[ROWS : ROWS + SHIFT, 0:COLS, :] = row_ref[which].astype(F32)
        ext_ref[0:ROWS, COLS : COLS + SHIFT, :] = col_ref[which].astype(F32)
        ext_ref[ROWS : ROWS + SHIFT, COLS : COLS + SHIFT, :] = corner_ref[which].astype(F32)
        pieces = []
        for wr in range(ROWS // WIN):
            for wc in range(COLS // WIN):
                r, c = WIN * wr + SHIFT, WIN * wc + SHIFT
                pieces.append(ext_ref[r : r + WIN, c : c + WIN, :].reshape(TOK, CHAN))
        return jnp.concatenate(pieces, axis=0)

    grad = windowed(g_ref, 1)
    grad_ref[...] = grad.astype(BF)
    grad_proj_bias = jnp.sum(grad, 0, keepdims=True)
    x = windowed(x_ref, 0)
    mean = jnp.sum(x, -1, keepdims=True) * (1.0 / CHAN)
    centered = x - mean
    rstd = lax.rsqrt(jnp.sum(centered * centered, -1, keepdims=True) * (1.0 / CHAN) + 1e-05)
    xhat = centered * rstd
    xhat_ref[...] = xhat
    rstd_ref[...] = rstd
    ls, lb, qb = rows_ref[0:1, 0:CHAN], rows_ref[1:2, 0:CHAN], rows_ref[2:3, :]
    normed = (xhat * ls + lb).astype(BF)
    normed_ref[...] = normed
    w_q, w_k, w_v = parts_ref[0], parts_ref[1], parts_ref[2]
    q_ref[...] = ((nn(normed, w_q) + qb[:, 0:CHAN]) * scale).astype(BF)
    k_ref[...] = (nn(normed, w_k) + qb[:, CHAN : 2 * CHAN]).astype(BF)
    v_ref[...] = (nn(normed, w_v) + qb[:, 2 * CHAN : 3 * CHAN]).astype(BF)
    da_ref[...] = nt(grad_ref[...], wp_ref[...]).astype(BF)

    head_of = iota((TOK, CHAN), 1) // DIM

    def by_head(a):
        zero = jnp.zeros_like(a)
        return jnp.concatenate([jnp.where(head_of == h, a, zero) for h in range(HEADS)], axis=0)

    def own_head(a):
        total = jnp.where(head_of == 0, a[0:TOK], 0.0)
        for h in range(1, HEADS):
            total = jnp.where(head_of == h, a[TOK * h : TOK * h + TOK], total)
        return total

    windows = [slice(TOK * win, TOK * win + TOK) for win in range(8)]
    for win, s in enumerate(windows):
        qh_ref[win] = by_head(q_ref[s])
        dah_ref[win] = by_head(da_ref[s])
    for win, s in enumerate(windows):
        apart = jnp.concatenate([apart_ref[win]] * 3, axis=1)
        p_ref[win] = nt(k_ref[s], qh_ref[win]) + bias_ref[...] + apart
        dp_ref[win] = nt(v_ref[s], dah_ref[win])
    d_sum = jnp.zeros((TOK, HEADS * TOK), F32)
    for win in range(8):
        scores = p_ref[win]
        e = jnp.exp(scores - jnp.max(scores, 0, keepdims=True))
        p = e * (1.0 / jnp.sum(e, 0, keepdims=True))
        pb_ref[win] = p.astype(BF)
        d_p = dp_ref[win]
        d_s = p * (d_p - jnp.sum(d_p * p, 0, keepdims=True))
        d_sum += d_s
        dsb_ref[win] = d_s.astype(BF)
    for win, s in enumerate(windows):
        attn_ref[s] = own_head(tn(pb_ref[win], v_ref[s])).astype(BF)
        dv_ref[s] = nn(pb_ref[win], dah_ref[win]).astype(BF)
        dq_ref[s] = (own_head(tn(dsb_ref[win], k_ref[s])) * scale).astype(BF)
        dk_ref[s] = nn(dsb_ref[win], qh_ref[win]).astype(BF)

    parts = [a for pair in range(3) for a in split(d_sum[:, 128 * pair : 128 * pair + 128])]
    spread = nn(jnp.concatenate(parts, axis=0), spread_pair())
    lines = []
    for pair in range(3):
        both = spread[128 * pair : 128 * pair + TOK] + spread[128 * pair + TOK : 128 * pair + 128]
        lines += [offset_sums(both[:, 0:128]), offset_sums(both[:, 128:256])]
    lines = jnp.concatenate(lines + [jnp.zeros((2, OFF), F32)], axis=0)
    high, low = split(lines)
    by_entry = nt(jnp.concatenate([high, low], axis=0), perm_ref[...])
    by_entry = by_entry[0:8] + by_entry[8:16]

    dq, dk, dv = dq_ref[...], dk_ref[...], dv_ref[...]
    d_normed = nt(dq, w_q) + nt(dk, w_k) + nt(dv, w_v)
    xhat = xhat_ref[...]
    norm_scale = jnp.sum(d_normed * xhat, 0, keepdims=True)
    norm_bias = jnp.sum(d_normed, 0, keepdims=True)
    dn_ref[...] = d_normed

    normed = normed_ref[...].T
    weights = jnp.concatenate(
        [nn(normed, dq), nn(normed, dk), nn(normed, dv), tn(attn_ref[...], grad_ref[...])], axis=1
    )
    sums = [jnp.sum(a.astype(F32), 0, keepdims=True) for a in (dq, dk, dv)] + [grad_proj_bias]
    small = jnp.concatenate(
        [
            jnp.concatenate(sums, axis=1),
            jnp.concatenate([norm_scale, norm_bias, jnp.zeros((1, 2 * CHAN), F32)], axis=1),
            jnp.concatenate([by_entry[0:1], by_entry[1:2], by_entry[2:3]], axis=1),
            jnp.concatenate([by_entry[3:4], by_entry[4:5], by_entry[5:6]], axis=1),
        ],
        axis=0,
    )
    high = small.astype(BF).astype(F32)
    small = jnp.concatenate([high, small - high], axis=0)
    packed = jnp.concatenate([weights, small], axis=0)
    for chunk in range(30):
        tiles = []
        for tile in range(5 * chunk, 5 * chunk + 5):
            r, c = tile // 6, tile % 6
            tiles.append(packed[8 * r : 8 * r + 8, 128 * c : 128 * c + 128])
        pack_ref[chunk] = jnp.concatenate(tiles, axis=0).astype(BF)
    pack_ref[30:CHUNKS] = jnp.zeros((CHUNKS - 30, PACK, 128), BF)


def add_up(ref, count):
    total = ref[0].astype(F32)
    for i in range(1, count):
        total += ref[i].astype(F32)
    return total


def part_sum(got_ref, place_ref):
    total = add_up(got_ref, got_ref.shape[0])
    tiles = []
    for i in range(PACK // 8):
        tile = total[8 * i : 8 * i + 8]
        whole = tile + pltpu.roll(tile, 4, 0)
        high = whole.astype(BF).astype(F32)
        parts = jnp.where(iota((8, 128), 0) < 4, high, whole - high)
        tiles.append(jnp.where(place_ref[0] * (PACK // 8) + i >= 6 * CHAN // 8, parts, tile))
    return jnp.concatenate(tiles, axis=0).astype(BF)


def finish_kernel(dn_ref, xhat_ref, rstd_ref, rows_ref, mark_ref, ds_ref, edge_ref):
    xhat = xhat_ref[...]
    d_hat = dn_ref[...] * rows_ref[0:1, 0:CHAN]
    mean_hat = jnp.sum(d_hat, -1, keepdims=True) * (1.0 / CHAN)
    mean_mix = jnp.sum(d_hat * xhat, -1, keepdims=True) * (1.0 / CHAN)
    d_shifted = rstd_ref[...] * (d_hat - mean_hat - xhat * mean_mix)
    for win in range(8):
        wr, wc = win // 4, win % 4
        block = d_shifted[TOK * win : TOK * win + TOK].reshape(WIN, WIN, CHAN)
        ds_ref[WIN * wr : WIN * wr + WIN, WIN * wc : WIN * wc + WIN, :] = block
    edge_ref[...] = ds_ref[ROWS - SHIFT : ROWS].astype(BF)


def sum_kernel(got_ref, place_ref, out_ref, mark_ref):
    mark_ref[...] = jnp.zeros_like(mark_ref)
    total = part_sum(got_ref, place_ref)
    for i in range(out_ref.shape[0]):
        out_ref[i] = total


def sum_edge_kernel(got_ref, above_ref, ds_ref, place_ref, out_ref, edge_ref):
    total = part_sum(got_ref, place_ref)
    for i in range(out_ref.shape[0]):
        out_ref[i] = total
    edge_ref[0:SHIFT] = above_ref[:, COLS - SHIFT : COLS]
    edge_ref[SHIFT:ROWS] = ds_ref[0 : ROWS - SHIFT, COLS - SHIFT : COLS].astype(BF)


def unpack_kernel(
    got_ref,
    g_ref,
    ds_ref,
    above_ref,
    left_ref,
    gx_ref,
    w_ref,
    wb_ref,
    p_ref,
    pb_ref,
    ns_ref,
    nb_ref,
    table_ref,
    all_ref,
    back_ref,
):
    back_ref[:, 0:SHIFT] = left_ref[...].astype(F32)
    back_ref[0:SHIFT, SHIFT:COLS] = above_ref[:, 0 : COLS - SHIFT].astype(F32)
    back_ref[SHIFT:ROWS, SHIFT:COLS] = ds_ref[0 : ROWS - SHIFT, 0 : COLS - SHIFT]
    gx_ref[...] = (g_ref[...].astype(F32) + back_ref[...]).astype(BF)
    for chunk in range(30):
        tiles = got_ref[chunk].astype(F32)
        for tile in range(5 * chunk, 5 * chunk + 5):
            r, c, part = tile // 6, tile % 6, 8 * (tile % 5)
            all_ref[8 * r : 8 * r + 8, 128 * c : 128 * c + 128] = tiles[part : part + 8]
    w_ref[...] = all_ref[0:CHAN, 0 : 3 * CHAN]
    p_ref[...] = all_ref[0:CHAN, 3 * CHAN : 4 * CHAN]
    small = all_ref[CHAN : CHAN + 4, :] + all_ref[CHAN + 4 : CHAN + 8, :]
    wb_ref[...] = small[0, 0 : 3 * CHAN]
    pb_ref[...] = small[0, 3 * CHAN : 4 * CHAN]
    ns_ref[...] = small[1, 0:CHAN]
    nb_ref[...] = small[1, CHAN : 2 * CHAN]
    for h in range(HEADS):
        place = OFF * (h % 3)
        table_ref[h : h + 1, :] = small[2 + h // 3 : 3 + h // 3, place : place + TABLE]


def kernel_call(kernel, out_shape, scratch=(), flops=10**7, **specs):
    return pl.pallas_call(
        kernel,
        out_shape=out_shape,
        scratch_shapes=scratch,
        **specs,
        cost_estimate=pl.CostEstimate(flops=flops, bytes_accessed=10**6, transcendentals=0),
        compiler_params=pltpu.CompilerParams(vmem_limit_bytes=40 * 2**20),
    )


def shape(dims, kind=F32):
    return jax.ShapeDtypeStruct(dims, kind)


def moved(block, axes, distance):
    sizes = [lax.axis_size(a) for a in axes]
    count = sizes[0] * sizes[1]
    return lax.ppermute(block, axes, [((i - distance) % count, i) for i in range(count)])


def moved_corner(block):
    pairs = [
        (8 * ((r + 1) % 8) + (c + 1) % 8, 8 * r + c) for r in range(8) for c in range(8)
    ]
    return lax.ppermute(block, ROW + COL, pairs)


def prepare(*args):
    return kernel_call(
        prepare_kernel,
        (
            shape((TOK, HEADS * TOK)),
            shape((OFF, OFF), BF),
            shape((8, TOK, 128)),
            shape((3, CHAN, CHAN), BF),
            shape((8, 3 * CHAN)),
        ),
    )(*args)


def halos(x, g):
    return kernel_call(
        halo_kernel,
        (
            shape((2, SHIFT, COLS, CHAN), BF),
            shape((2, SHIFT, SHIFT, CHAN), BF),
        ),
    )(x, g)


def main(*args):
    tokens = 8 * TOK
    return kernel_call(
        main_kernel,
        (
            shape((tokens, CHAN)),
            shape((tokens, CHAN)),
            shape((tokens, 1)),
            shape((CHUNKS, PACK, 128), BF),
        ),
        [
            pltpu.VMEM((ROWS + 8, COLS + 8, CHAN), F32),
        ]
        + [pltpu.VMEM((tokens, CHAN), BF)] * 10
        + [pltpu.VMEM((8, HEADS * TOK, CHAN), BF)] * 2
        + [pltpu.VMEM((8, TOK, HEADS * TOK), F32)] * 2
        + [pltpu.VMEM((8, TOK, HEADS * TOK), BF)] * 2,
        flops=10**9,
    )(*args)


SMALL = pl.BlockSpec(memory_space=pltpu.SMEM)
WHOLE = pl.BlockSpec(memory_space=pltpu.VMEM)


def chunk_sum(got, copies, place):
    return kernel_call(
        sum_kernel,
        (shape((copies,) + got.shape[1:], BF), shape((8, 128))),
        in_specs=[WHOLE, SMALL],
    )(got, place)


def finish(*args):
    return kernel_call(
        finish_kernel, (shape((ROWS, COLS, CHAN)), shape((SHIFT, COLS, CHAN), BF))
    )(*args)


def chunk_sum_edge(got, copies, above, d_shifted, place):
    return kernel_call(
        sum_edge_kernel,
        (shape((copies,) + got.shape[1:], BF), shape((ROWS, SHIFT, CHAN), BF)),
        in_specs=[WHOLE, WHOLE, WHOLE, SMALL],
    )(got, above, d_shifted, place)


def unpack(*args):
    return kernel_call(
        unpack_kernel,
        (
            shape((ROWS, COLS, CHAN), BF),
            shape((CHAN, 3 * CHAN)),
            shape((3 * CHAN,)),
            shape((CHAN, CHAN)),
            shape((CHAN,)),
            shape((CHAN,)),
            shape((CHAN,)),
            shape((HEADS, TABLE)),
        ),
        [pltpu.VMEM((CHAN + 8, 4 * CHAN), F32), pltpu.VMEM((ROWS, COLS, CHAN), F32)],
    )(*args)


def on_device(
    block_input,
    grad_out,
    region_ids,
    layernorm_scale,
    layernorm_bias,
    qkv_weight,
    qkv_bias,
    proj_weight,
    bias_table,
    position_index,
):
    x, g = block_input[0], grad_out[0]
    col = moved(jnp.stack([x[:, :SHIFT], g[:, :SHIFT]]), COL, -1)
    row, corner = halos(x, g)
    row, corner = moved(row, ROW, -1), moved_corner(corner)
    bias, perm, apart, parts, rows = prepare(
        position_index, bias_table.T, region_ids, qkv_weight, layernorm_scale, layernorm_bias, qkv_bias
    )
    place = lax.axis_index(FIRST).astype(jnp.int32)[None]
    rows, place = lax.optimization_barrier((rows, place))
    d_normed, xhat, rstd, packed = main(
        x, g, row, col, corner, parts, proj_weight, bias, perm, apart, rows
    )
    got = lax.all_to_all(packed, FIRST, 0, 0, tiled=True)
    part, mark = chunk_sum(got, 16, place)
    d_shifted, edge = finish(d_normed, xhat, rstd, rows, mark)
    above = moved(edge, ROW, 1)
    got = lax.all_to_all(part, SECOND, 0, 0, tiled=True)
    whole, edge = chunk_sum_edge(got, CHUNKS, above, d_shifted, place)
    left = moved(edge, COL, 1)
    gathered = lax.all_to_all(whole, FIRST, 0, 0, tiled=True)
    grad_x, w, wb, p, pb, ns, nb, table = unpack(gathered, g, d_shifted, above, left)
    return (grad_x[None], w, wb, p, pb, ns, nb, table.T)


def solution(mesh):
    fine = Mesh(mesh.devices.reshape(8, 4, 2, 2, 4), ("y", "zl", "c", "zh", "x"))
    tiles = P("y", ROW, COL, None)
    return jax.shard_map(
        on_device,
        mesh=fine,
        in_specs=(tiles, tiles, P(ROW, COL), P(), P(), P(), P(), P(), P(), P()),
        out_specs=(tiles, P(), P(), P(), P(), P(), P(), P()),
        check_vma=False,
    )
```
